32 devices in a mesh: head: 4 (over x, core), blk: 8 (over z, y).
Axes of the slice: x: 2, y: 2, z: 4, core: 2. Of those that a mesh axis runs over, the one named last changes fastest.
Arguments:
- inputs: bfloat16 [1536, 1, 3072], P('blk', None, 'head'), may hold values from -17.5 to 17.5
- out_grad: bfloat16 [1536, 1, 3072], P('blk', None, 'head'), may hold values from -6 to 6
- qkv_weight: bfloat16 [3072, 3, 1536], P(None, None, 'head'), may hold values from -0.108253175 to 0.108253175
- out_weight: bfloat16 [3072, 1536], P(None, 'head'), may hold values from -0.15625 to 0.15625
- text_keys: bfloat16 [256, 1, 1536], P(None, None, 'head'), may hold values from -6 to 6
- text_values: bfloat16 [256, 1, 1536], P(None, None, 'head'), may hold values from -6 to 6
- text_mask: int32 [256, 1], replicated, may hold values 0 or 1
Outputs:
- grad_inputs: bfloat16 [1536, 1, 3072], P('blk', None, 'head')
- grad_qkv_weight: float32 [3072, 3, 1536], P('blk', None, 'head')
- grad_out_weight: float32 [3072, 1536], P('blk', 'head')
- grad_text_keys: float32 [256, 1, 1536], P('blk', None, 'head')
- grad_text_values: float32 [256, 1, 1536], P('blk', None, 'head')
The draws below stay inside these ranges and needn't reach their ends.
All inputs are finite; a program needn't handle non-finite values.
Results may differ from the reference program's by a relative error of at most 0.034.
Values may be sent and summed in bfloat16 or wider, within the bound.
A program may use at most 128 MiB of HBM per device.

```python
import jax
import jax.numpy as jnp
from jax import lax

D = 3072
HD = 128
TXT = 256
SEQS = 1
VID_DEV = 192
HEADS = 12
VIDEO = 1536
N_BLK = 8


def draw_inputs(key, part):
    key = jax.random.fold_in(key, 11)
    shape = (VIDEO, SEQS, D)
    values = jnp.clip(jax.random.normal(key, shape, jnp.float32), -6.0, 6.0)
    return values.astype(jnp.bfloat16)


def draw_qkv_weight(key, part):
    key = jax.random.fold_in(key, 31)
    shape = (D, 3, HEADS * HD)
    scale = D ** (-0.5)
    values = jnp.clip(jax.random.normal(key, shape, jnp.float32), -6.0, 6.0) * scale
    return values.astype(jnp.bfloat16)


def place_ends(drawn, key, least, high):
    longest = drawn.shape.index(max(drawn.shape))
    spots = []
    for shift in (0, 1):
        where = [jax.random.randint(jax.random.fold_in(key, axis), (), 0, length) for axis, length in enumerate(drawn.shape)]
        where[longest] = (where[longest] + shift) % drawn.shape[longest]
        spots.append(tuple(where))
    return drawn.at[spots[0]].set(least).at[spots[1]].set(high)


def strengthened(drawn, key, source, target, parts, factor):
    def block_of(dim):
        return (jnp.arange(drawn.shape[dim]) // (drawn.shape[dim] // parts)).reshape((-1,) + (1,) * (drawn.ndim - 1 - dim))

    one_side = jax.random.permutation(key, parts)[block_of(target)]
    second = (block_of(target) + parts // 2) % parts
    return jnp.where((block_of(source) == one_side) | (block_of(source) == second), factor * drawn, drawn)


def level_of(rng, extent, cuts, least, high):
    level = 1.0
    for dim, parts in cuts:
        steps = jax.random.uniform(jax.random.fold_in(jax.random.fold_in(rng, 6), dim), (parts,), jnp.float32, least / len(cuts), high / len(cuts))
        level = level * jnp.repeat(jnp.exp(steps), extent[dim] // parts).reshape((-1,) + (1,) * (len(extent) - 1 - dim))
    return level


def scatter_about(key, extent, deviation, reach, split=(), kind=jnp.bfloat16):
    factor_of = level_of(key, extent, split, -0.22, 0.18) if split else 1.0
    values = jax.random.normal(key, extent, jnp.float32) * deviation * factor_of
    return jnp.minimum(jnp.maximum(values, -reach), reach).astype(kind)


def noise_with(key, extent, scale, reach, cuts, heavy, kind=jnp.bfloat16):
    array = scale * jax.random.normal(key, extent, jnp.float32)
    if cuts:
        array = array * level_of(key, extent, cuts, -0.22, 0.18)
    return jnp.clip(strengthened(array, jax.random.fold_in(key, 3), *heavy), -reach, reach).astype(kind)


def setup_inputs(seed: int = 0) -> dict:
    splits = jax.random.split(jax.random.key(seed), 8)
    return {
        "inputs": draw_inputs(jax.random.fold_in(splits[7], 71), 0),
        "out_grad": noise_with(splits[1], (VIDEO, SEQS, D), 1.0, 6.0, ((0, 8), (2, 4)), (0, 2, 8, 2.0)),
        "qkv_weight": draw_qkv_weight(jax.random.fold_in(splits[7], 71), 0),
        "out_weight": scatter_about(splits[3], (D, HEADS * HD), (HEADS * HD) ** -0.5, 0.15625, ((1, 4),)),
        "text_keys": scatter_about(splits[4], (TXT, SEQS, HEADS * HD), 1.0, 6.0, ((2, 4),)),
        "text_values": scatter_about(splits[5], (TXT, SEQS, HEADS * HD), 1.0, 6.0, ((2, 4),)),
        "text_mask": place_ends((jax.random.randint(splits[6], (TXT, SEQS), 0, 4) < 3).astype(jnp.int32), jax.random.fold_in(splits[6], 1), 0, 1),
    }


masked_fill = -1.0e9


def settle(values):
    return lax.optimization_barrier(values.astype(jnp.bfloat16)).astype(jnp.float32)


def reference(inputs, out_grad, qkv_weight, out_weight, text_keys, text_values, text_mask):
    model_width = HEADS * HD
    score_scale = HD ** -0.5
    total_rows = VIDEO * SEQS
    flat_inputs = inputs.reshape(total_rows, D)
    flat_grads = out_grad.reshape(total_rows, D)
    projected = jnp.dot(flat_inputs, qkv_weight.reshape(D, 3 * model_width), preferred_element_type=jnp.float32)
    projected = projected.astype(jnp.bfloat16).reshape(VIDEO, SEQS, 3, HEADS, HD)
    grad_attn = jnp.dot(flat_grads, out_weight, preferred_element_type=jnp.float32)
    grad_attn = grad_attn.astype(jnp.bfloat16).reshape(VIDEO, SEQS, HEADS, HD)
    text_valid = text_mask == 1
    key_valid = jnp.concatenate([text_valid, jnp.ones((VIDEO, SEQS), dtype=bool)], axis=0)
    head_items = (
        jnp.transpose(projected[:, :, 0], (2, 0, 1, 3)),
        jnp.transpose(projected[:, :, 1], (2, 0, 1, 3)),
        jnp.transpose(projected[:, :, 2], (2, 0, 1, 3)),
        jnp.transpose(grad_attn, (2, 0, 1, 3)),
        jnp.transpose(text_keys.reshape(TXT, SEQS, HEADS, HD), (2, 0, 1, 3)),
        jnp.transpose(text_values.reshape(TXT, SEQS, HEADS, HD), (2, 0, 1, 3)),
    )

    def one_head(head_arrays):
        query_all, key_video, value_video, grad_all, key_text, value_text = head_arrays
        key_rows = jnp.concatenate([key_text, key_video], axis=0).astype(jnp.float32)
        value_rows = jnp.concatenate([value_text, value_video], axis=0).astype(jnp.float32)
        valid_mask = key_valid.T[:, None, :]

        def per_block(sums, block_index):
            text_sum, video_sum = sums
            first_row = (block_index * VID_DEV).astype(jnp.int32)
            query_block = lax.dynamic_slice_in_dim(query_all, first_row, VID_DEV, 0).astype(jnp.float32)
            grad_block = lax.dynamic_slice_in_dim(grad_all, first_row, VID_DEV, 0).astype(jnp.float32)
            logits = jnp.einsum("vsd,lsd->svl", query_block, key_rows) * score_scale
            logits = jnp.where(valid_mask, logits, masked_fill)
            row_max = jnp.max(logits, axis=-1)
            raw_weights = jnp.exp(logits - row_max[..., None])
            total = jnp.sum(raw_weights, axis=-1)
            out_block = jnp.einsum("svl,lsd->vsd", settle(raw_weights), value_rows) / total.T[:, :, None]
            out_block = out_block.astype(jnp.bfloat16)
            log_total = row_max + jnp.log(total)
            row_dot = jnp.sum(grad_block * out_block.astype(jnp.float32), axis=-1)
            probabilities = jnp.exp(logits - log_total[..., None])
            grad_values = jnp.einsum("svl,vsd->lsd", settle(probabilities), grad_block)
            grad_probs = jnp.einsum("vsd,lsd->svl", grad_block, value_rows)
            grad_logits = settle(probabilities * (grad_probs - row_dot.T[..., None]) * score_scale)
            grad_query = jnp.einsum("svl,lsd->vsd", grad_logits, key_rows).astype(jnp.bfloat16)
            grad_keys = jnp.einsum("svl,vsd->lsd", grad_logits, query_block)
            key_term = jnp.stack([grad_keys, grad_values], axis=2)
            text_sum = text_sum + key_term[:TXT]
            video_sum = video_sum + settle(key_term[TXT:])
            return (text_sum, video_sum), (grad_query, out_block)

        start_sums = (jnp.zeros((TXT, SEQS, 2, HD), jnp.float32), jnp.zeros((VIDEO, SEQS, 2, HD), jnp.float32))
        final_sums, block_outputs = lax.scan(per_block, start_sums, jnp.arange(N_BLK, dtype=jnp.int32))
        grad_query = block_outputs[0].reshape(VIDEO, SEQS, HD)
        out_rows = block_outputs[1].reshape(VIDEO, SEQS, HD)
        return grad_query, out_rows, final_sums[0], final_sums[1].astype(jnp.bfloat16)

    grad_query, out_rows, text_sum, video_sum = lax.map(one_head, head_items)
    grad_query = jnp.transpose(grad_query, (1, 2, 0, 3)).reshape(VIDEO, SEQS, 1, model_width)
    attn_out = jnp.transpose(out_rows, (1, 2, 0, 3)).reshape(VIDEO, SEQS, model_width)
    video_kv = jnp.transpose(video_sum, (1, 2, 3, 0, 4)).reshape(VIDEO, SEQS, 2, model_width)
    text_kv = jnp.transpose(text_sum, (1, 2, 3, 0, 4)).reshape(TXT, SEQS, 2, model_width)
    grad_projected = jnp.concatenate([grad_query, video_kv], axis=2)
    flat_projected = grad_projected.reshape(total_rows, 3 * model_width)
    grad_inputs = jnp.dot(flat_projected, qkv_weight.reshape(D, 3 * model_width).T, preferred_element_type=jnp.float32)
    grad_inputs = grad_inputs.astype(jnp.bfloat16).reshape(VIDEO, SEQS, D)

    def weight_block(sums, block_index):
        qkv_sum, out_sum = sums
        first_row = (block_index * VID_DEV).astype(jnp.int32)
        input_block = lax.dynamic_slice_in_dim(inputs, first_row, VID_DEV, 0).reshape(VID_DEV * SEQS, D)
        grad_block = lax.dynamic_slice_in_dim(out_grad, first_row, VID_DEV, 0).reshape(VID_DEV * SEQS, D)
        projected_block = lax.dynamic_slice_in_dim(grad_projected, first_row, VID_DEV, 0).reshape(VID_DEV * SEQS, 3 * model_width)
        attn_block = lax.dynamic_slice_in_dim(attn_out, first_row, VID_DEV, 0).reshape(VID_DEV * SEQS, model_width)
        qkv_sum = qkv_sum + settle(jnp.dot(input_block.T, projected_block, preferred_element_type=jnp.float32))
        out_sum = out_sum + settle(jnp.dot(grad_block.T, attn_block, preferred_element_type=jnp.float32))
        return (qkv_sum, out_sum), None

    start_weights = (jnp.zeros((D, 3 * model_width), jnp.float32), jnp.zeros((D, model_width), jnp.float32))
    weight_sums, unused = lax.scan(weight_block, start_weights, jnp.arange(N_BLK, dtype=jnp.int32))
    grad_qkv_weight = weight_sums[0].reshape(D, 3, model_width)
    grad_out_weight = weight_sums[1]
    return grad_inputs, grad_qkv_weight, grad_out_weight, text_kv[:, :, 0], text_kv[:, :, 1]
```

```python
import functools

import jax
import jax.numpy as jnp
from jax import lax
from jax.experimental import pallas as pl
from jax.experimental.pallas import tpu as pltpu
from jax.sharding import PartitionSpec as P

HD = 128


masked_fill = -1000000000.0


def masked_logits(query_heads, key_rows, valid_rows, score_scale):
    logits = (
        jnp.einsum("vsne,jsne->snvj", query_heads, key_rows, preferred_element_type=jnp.float32)
        * score_scale
    )
    if valid_rows is not None:
        logits = jnp.where(valid_rows.T[:, None, None, :], logits, masked_fill)
    return logits


def attend_block(softmax_state, query_heads, key_rows, value_rows, valid_rows, score_scale):
    running_max, running_sum, running_acc = softmax_state
    logits = masked_logits(query_heads, key_rows, valid_rows, score_scale)
    new_max = jnp.maximum(running_max, jnp.max(logits, axis=-1))
    factor = jnp.exp(running_max - new_max)
    weights = jnp.exp(logits - new_max[..., None])
    new_sum = running_sum * factor + jnp.sum(weights, axis=-1)
    update = jnp.einsum(
        "snvj,jsne->snve",
        weights.astype(jnp.bfloat16),
        value_rows,
        preferred_element_type=jnp.float32,
    )
    return (new_max, new_sum, running_acc * factor[..., None] + update)


def grad_block(
    query_heads, grad_heads, key_rows, value_rows, valid_rows, log_total, row_dot, score_scale
):
    logits = masked_logits(query_heads, key_rows, valid_rows, score_scale)
    probabilities = jnp.exp(logits - log_total[..., None])
    grad_values = jnp.einsum(
        "snvj,vsne->jsne",
        probabilities.astype(jnp.bfloat16),
        grad_heads,
        preferred_element_type=jnp.float32,
    )
    grad_probs = jnp.einsum(
        "vsne,jsne->snvj", grad_heads, value_rows, preferred_element_type=jnp.float32
    )
    grad_logits = (probabilities * (grad_probs - row_dot[..., None]) * score_scale).astype(
        jnp.bfloat16
    )
    grad_queries = jnp.einsum(
        "snvj,jsne->vsne", grad_logits, key_rows, preferred_element_type=jnp.float32
    )
    grad_keys = jnp.einsum(
        "snvj,vsne->jsne", grad_logits, query_heads, preferred_element_type=jnp.float32
    )
    return (grad_queries, jnp.stack([grad_keys, grad_values], axis=2))


def key_blocks(full_kv, shard_rows, shards, seq_count, head_count, head_dim):
    group_size = 1
    while group_size * shard_rows < 512 and group_size < shards:
        group_size = group_size * 2
    return full_kv.reshape(
        shards // group_size, group_size * shard_rows, seq_count, 2, head_count, head_dim
    )


def plain_device(inputs, out_grad, qkv_weight, out_weight, text_keys, text_values, text_mask):
    full_in, full_grad = (
        lax.all_gather(inputs, "head", axis=2, tiled=True),
        lax.all_gather(out_grad, "head", axis=2, tiled=True),
    )
    shard_rows = inputs.shape[0]
    seq_count = inputs.shape[1]
    local_width = qkv_weight.shape[2]
    head_dim = HD
    head_count = local_width // head_dim
    score_scale = head_dim ** (-0.5)
    shards = lax.axis_size("blk")
    projected = jnp.einsum(
        "vsd,dch->vsch", full_in, qkv_weight, preferred_element_type=jnp.float32
    ).astype(jnp.bfloat16)
    grad_attn = jnp.einsum(
        "vsd,dh->vsh", full_grad, out_weight, preferred_element_type=jnp.float32
    ).astype(jnp.bfloat16)
    query_heads = projected[:, :, 0].reshape(shard_rows, seq_count, head_count, head_dim)
    grad_heads = grad_attn.reshape(shard_rows, seq_count, head_count, head_dim)
    kv_local = projected[:, :, 1:]
    text_rows = text_keys.shape[0]
    valid_text = text_mask == 1
    text_key_heads = text_keys.reshape(text_rows, seq_count, head_count, head_dim)
    text_value_heads = text_values.reshape(text_rows, seq_count, head_count, head_dim)
    start_state = (
        jnp.full((seq_count, head_count, shard_rows), -1e30, jnp.float32),
        jnp.zeros((seq_count, head_count, shard_rows), jnp.float32),
        jnp.zeros((seq_count, head_count, shard_rows, head_dim), jnp.float32),
    )
    softmax_state = attend_block(
        start_state, query_heads, text_key_heads, text_value_heads, valid_text, score_scale
    )
    kv_piece = lax.all_gather(kv_local, "blk", axis=0, tiled=True)
    key_slice = kv_piece.reshape(kv_piece.shape[0], seq_count, 2, head_count, head_dim)
    softmax_state = attend_block(
        softmax_state, query_heads, key_slice[:, :, 0], key_slice[:, :, 1], None, score_scale
    )
    run_max, run_sum, run_acc = softmax_state
    out_heads = jnp.transpose(run_acc / run_sum[..., None], (2, 0, 1, 3)).astype(jnp.bfloat16)
    attn_out = out_heads.reshape(shard_rows, seq_count, local_width)
    log_total = run_max + jnp.log(run_sum)
    row_dot = jnp.transpose(
        jnp.sum(grad_heads.astype(jnp.float32) * out_heads.astype(jnp.float32), axis=-1), (1, 2, 0)
    )
    text_query_grads, text_terms = grad_block(
        query_heads,
        grad_heads,
        text_key_heads,
        text_value_heads,
        valid_text,
        log_total,
        row_dot,
        score_scale,
    )
    text_sums = lax.psum_scatter(
        text_terms.reshape(text_rows, seq_count, 2, local_width).astype(jnp.bfloat16),
        "blk",
        scatter_dimension=0,
        tiled=True,
    ).astype(jnp.float32)
    full_kv = lax.all_gather(kv_local, "blk", axis=0, tiled=True)
    blocks = key_blocks(full_kv, shard_rows, shards, seq_count, head_count, head_dim)

    def backward_step(running, kv_block):
        partial_value, key_term = grad_block(
            query_heads,
            grad_heads,
            kv_block[:, :, 0],
            kv_block[:, :, 1],
            None,
            log_total,
            row_dot,
            score_scale,
        )
        return (running + partial_value, key_term)

    query_grads, key_terms = lax.scan(backward_step, text_query_grads, blocks)
    key_terms = key_terms.reshape(full_kv.shape[0], seq_count, 2, local_width)
    kv_grads = lax.psum_scatter(
        key_terms.astype(jnp.bfloat16), "blk", scatter_dimension=0, tiled=True
    )
    grad_projected = jnp.concatenate(
        [query_grads.astype(jnp.bfloat16).reshape(shard_rows, seq_count, 1, local_width), kv_grads],
        axis=2,
    )
    input_terms = jnp.einsum(
        "vsch,dch->vsd", grad_projected, qkv_weight, preferred_element_type=jnp.float32
    )
    grad_inputs = lax.psum_scatter(
        input_terms.astype(jnp.bfloat16), "head", scatter_dimension=2, tiled=True
    )
    qkv_part = jnp.einsum(
        "vsd,vsch->dch", full_in, grad_projected, preferred_element_type=jnp.float32
    )
    out_part = jnp.einsum("vsd,vsh->dh", full_grad, attn_out, preferred_element_type=jnp.float32)
    weight_grads = lax.psum_scatter(
        jnp.concatenate([qkv_part, out_part[:, None]], axis=1).astype(jnp.bfloat16),
        "blk",
        scatter_dimension=0,
        tiled=True,
    ).astype(jnp.float32)
    return (
        grad_inputs,
        weight_grads[:, :3],
        weight_grads[:, 3],
        text_sums[:, :, 0],
        text_sums[:, :, 1],
    )


MESH = pl.DeviceIdType.MESH
LOG2E = 1.4426950408889634
VMEM_BYTES = 60 * 1024 * 1024


def dot(a, b, contract=((1,), (0,))):
    return lax.dot_general(a, b, (contract, ((), ())), preferred_element_type=jnp.float32)


def fused_kernel(
    n,
    tile,
    x_hbm,
    g_hbm,
    wqkv_hbm,
    wout_hbm,
    tk_ref,
    tv_ref,
    mask_ref,
    dx_ref,
    dwqkv_ref,
    dwout_ref,
    dtk_ref,
    dtv_ref,
    full,
    weights,
    proj,
    ring,
    cols_in,
    cols_t,
    keys,
    values,
    keys_t,
    values_t,
    grad_k,
    grad_v,
    gp,
    pair_out,
    pair_in,
    cross_out,
    cross_in,
    load_sem,
    head_send,
    head_recv,
    ring_send,
    ring_recv,
    own_sem,
    swap_send,
    swap_recv,
    col_send,
    col_recv,
    red_send,
    red_recv,
):
    rows, depth = full.shape[1], full.shape[2]
    feats = x_hbm.shape[1]
    heads = ring.shape[0]
    text = tk_ref.shape[0]
    total_rows = ring.shape[2]
    width = cols_in.shape[3]
    quarter = rows // 4
    tiles = total_rows // tile
    half = n // 2
    scale = HD ** (-0.5)

    hd = lax.axis_index("head")
    me = lax.axis_index("blk")
    sib = hd + 1 - 2 * (hd % 2)
    far = (hd + 2) % 4
    diag = (sib + 2) % 4
    odd = me % 2
    pos = (1 - odd) * (me // 2) + odd * (n - 1 - me // 2)

    def blk_at(p):
        p = p % n
        hi = p // half
        return (1 - hi) * (2 * p) + hi * (2 * (n - 1 - p) + 1)

    right, left = blk_at(pos + 1), blk_at(pos + n - 1)

    def feat(j):
        return pl.ds(pl.multiple_of(j * feats, 128), feats)

    def block(j):
        return pl.ds(pl.multiple_of(j * rows, 16), rows)

    w_loads = [
        pltpu.make_async_copy(wqkv_hbm, weights.at[pl.ds(0, 3)], load_sem.at[2]),
        pltpu.make_async_copy(wout_hbm, weights.at[3], load_sem.at[3]),
    ]
    own_loads = [
        pltpu.make_async_copy(src, full.at[a, :, feat(hd)], load_sem.at[a])
        for a, src in enumerate((x_hbm, g_hbm))
    ]
    for c in own_loads + w_loads:
        c.start()

    barrier = pltpu.get_barrier_semaphore()
    for r in range(1, n):
        pl.semaphore_signal(
            barrier, inc=1, device_id={"blk": (me + r) % n}, device_id_type=MESH
        )
    for other in (sib, far):
        pl.semaphore_signal(barrier, inc=1, device_id={"head": other}, device_id_type=MESH)
    pl.semaphore_wait(barrier, n + 1)

    def head_copy(a, kind):
        j = far if kind == 2 else hd
        ref = full.at[a, :, feat(j)]
        return pltpu.make_async_remote_copy(
            src_ref=ref,
            dst_ref=ref,
            send_sem=head_send.at[a, kind],
            recv_sem=head_recv.at[a, kind],
            device_id={"head": far if kind == 0 else sib},
            device_id_type=MESH,
        )

    for a in range(2):
        own_loads[a].wait()
        head_copy(a, 0).start()
        head_copy(a, 1).start()

    def project(a, j, first=False):
        part = full[a, :, feat(j)]
        for c in (0, 1, 2) if a == 0 else (3,):
            term = dot(part, weights[c, feat(j), :])
            proj[c] = term if first else proj[c] + term

    for c in w_loads:
        c.wait()
    for a in range(2):
        project(a, hd, True)
    for a in range(2):
        head_copy(a, 1).wait_recv()
        project(a, sib)
    for a in range(2):
        head_copy(a, 0).wait_recv()
        head_copy(a, 2).start()
        project(a, far)
    for a in range(2):
        head_copy(a, 2).wait_recv()
        project(a, diag)
    for h in range(heads):
        for c in range(4):
            ring[h, c, block(me), :] = proj[c, :, h * HD : (h + 1) * HD].astype(jnp.bfloat16)

    def ring_copy(h, s, way):
        p = pos - (s - 1) + n if way == 0 else pos + s - 1
        j = blk_at(p)
        if s < half:
            ref = ring.at[h, :, block(j), :]
        else:
            ref = ring.at[h, pl.ds(2 * way, 2), block(j), :]
        return pltpu.make_async_remote_copy(
            src_ref=ref,
            dst_ref=ref,
            send_sem=ring_send.at[h, s - 1, way],
            recv_sem=ring_recv.at[h, s - 1, way],
            device_id={"blk": right if way == 0 else left},
            device_id_type=MESH,
        )

    def hop(h, s):
        for way in range(2):
            if s > 1:
                ring_copy(h, s - 1, way).wait_recv()
            ring_copy(h, s, way).start()

    def finish(h):
        for way in range(2):
            ring_copy(h, half, way).wait_recv()
            for s in range(1, half + 1):
                ring_copy(h, s, way).wait_send()

    mine = pl.ds(pl.multiple_of(hd * quarter, 16), quarter)

    def wide(j):
        return pl.ds(pl.multiple_of(j * width, 128), width)

    def swap_copy(r):
        to = (me + r) % n
        return pltpu.make_async_remote_copy(
            src_ref=full.at[:, mine, wide(to)],
            dst_ref=cols_in.at[:, me, mine, :],
            send_sem=swap_send.at[r],
            recv_sem=swap_recv.at[r],
            device_id={"blk": to},
            device_id_type=MESH,
        )

    own_cols = pltpu.make_async_copy(
        full.at[:, mine, wide(me)], cols_in.at[:, me, mine, :], own_sem.at[0]
    )

    def swap_start():
        own_cols.start()
        for r in range(1, n):
            swap_copy(r).start()

    def col_copy(kind):
        j = far if kind == 2 else hd
        ref = cols_in.at[:, :, pl.ds(pl.multiple_of(j * quarter, 16), quarter), :]
        return pltpu.make_async_remote_copy(
            src_ref=ref,
            dst_ref=ref,
            send_sem=col_send.at[kind],
            recv_sem=col_recv.at[kind],
            device_id={"head": far if kind == 0 else sib},
            device_id_type=MESH,
        )

    def cols_start():
        own_cols.wait()
        for r in range(1, n):
            swap_copy(r).wait_recv()
        col_copy(0).start()
        col_copy(1).start()

    def cols_forward():
        col_copy(0).wait_recv()
        col_copy(2).start()

    def attend(h, events):
        lanes = pl.ds(h * HD, HD)
        keys[pl.ds(0, text), :] = tk_ref[:, lanes]
        keys[pl.ds(text, total_rows), :] = ring[h, 1]
        values[pl.ds(0, text), :] = tv_ref[:, lanes]
        values[pl.ds(text, total_rows), :] = ring[h, 2]
        keys_t[...] = keys[...].T
        values_t[...] = values[...].T
        grad_k[...] = jnp.zeros_like(grad_k)
        grad_v[...] = jnp.zeros_like(grad_v)

        @pl.loop(0, tiles)
        def _(i):
            for at, run in events:
                pl.when(i == at)(run)
            here = pl.ds(pl.multiple_of(i * tile, tile), tile)
            q = ring[h, 0, here, :]
            go = ring[h, 3, here, :]
            go_t = go.T
            logits = dot(keys[...], q.T)
            logits = jnp.concatenate(
                [jnp.where(mask_ref[...] > 0.0, logits[:text], masked_fill / scale), logits[text:]],
                axis=0,
            )
            top = jnp.max(logits, axis=0, keepdims=True)
            p = jnp.exp2((logits - top) * (scale * LOG2E))
            inv = 1.0 / jnp.sum(p, axis=0, keepdims=True)
            pb = p.astype(jnp.bfloat16)
            out_t = (dot(values_t[...], pb) * inv).astype(jnp.bfloat16)
            go_f = go_t.astype(jnp.float32)
            row_dot = jnp.sum(go_f * out_t.astype(jnp.float32), axis=0, keepdims=True)
            gp_t = dot(values[...], go_t)
            ds = (p * ((gp_t - row_dot) * (inv * scale))).astype(jnp.bfloat16)
            dq_t = dot(keys_t[...], ds)
            grad_k[...] += dot(ds, q)
            grad_v[...] += dot(pb, (go_f * inv).astype(jnp.bfloat16).T)
            ring[h, 0, here, :] = dq_t.astype(jnp.bfloat16).T
            ring[h, 3, here, :] = out_t.T

        ring[h, 1] = grad_k[pl.ds(text, total_rows), :].astype(jnp.bfloat16)
        ring[h, 2] = grad_v[pl.ds(text, total_rows), :].astype(jnp.bfloat16)
        part = text // n
        own_text = pl.ds(pl.multiple_of(me * part, 8), part)
        dtk_ref[:, lanes] = grad_k[own_text, :]
        dtv_ref[:, lanes] = grad_v[own_text, :]

    order = []
    for h in range(heads):
        order += [(h, s) for s in range(2 if h else 1, half)]
        if h + 1 < heads:
            order.append((h + 1, 1))
        order.append((h, half))
    for h, s in order[: half + 1]:
        hop(h, s)
    rest = order[half + 1 :]
    for h in range(heads):
        finish(h)
        if h + 1 < heads:
            todo = [functools.partial(hop, *e) for e in rest[:half]] if h + 2 < heads else [
                functools.partial(hop, *e) for e in rest
            ]
            rest = rest[half:]
            if h + 2 == heads:
                todo.append(swap_start)
        else:
            todo = [cols_start, cols_forward]
        if h + 1 < heads:
            events = [(min(tiles - 1, e * tiles // len(todo)), run) for e, run in enumerate(todo)]
        else:
            events = [(tiles // 2, todo[0]), (tiles - 1, todo[1])]
        attend(h, events)

    for h in range(heads):
        for c in range(3):
            gp[c, :, pl.ds(h * HD, HD)] = ring[h, c, block(me), :]

    def input_term(j):
        return sum(dot(gp[c], weights[c, feat(j), :], ((1,), (1,))) for c in range(3))

    def pair_copy(k):
        return pltpu.make_async_remote_copy(
            src_ref=pair_out.at[k],
            dst_ref=pair_in.at[k],
            send_sem=red_send.at[k],
            recv_sem=red_recv.at[k],
            device_id={"head": sib},
            device_id_type=MESH,
        )

    cross_copy = pltpu.make_async_remote_copy(
        src_ref=cross_out,
        dst_ref=cross_in,
        send_sem=red_send.at[2],
        recv_sem=red_recv.at[2],
        device_id={"head": far},
        device_id_type=MESH,
    )
    pair_out[1] = input_term(diag).astype(jnp.bfloat16)
    pair_copy(1).start()
    pair_out[0] = input_term(sib).astype(jnp.bfloat16)
    pair_copy(0).start()
    far_term = input_term(far)
    pair_copy(1).wait_recv()
    cross_out[...] = (far_term + pair_in[1].astype(jnp.float32)).astype(jnp.bfloat16)
    cross_copy.start()
    own_term = input_term(hd)
    pair_copy(0).wait_recv()
    own_term = own_term + pair_in[0].astype(jnp.float32)

    col_copy(1).wait_recv()
    col_copy(2).wait_recv()
    for a in range(2):
        cols_t[a] = cols_in[a].reshape(total_rows, width).T
    for h in range(heads):
        lanes = pl.ds(h * HD, HD)
        three = jnp.concatenate([ring[h, 0], ring[h, 1], ring[h, 2]], axis=1)
        term = dot(cols_t[0], three)
        for c in range(3):
            dwqkv_ref[c, :, lanes] = term[:, c * HD : (c + 1) * HD]
        dwout_ref[:, lanes] = dot(cols_t[1], ring[h, 3])

    cross_copy.wait_recv()
    dx_ref[...] = (own_term + cross_in[...].astype(jnp.float32)).astype(jnp.bfloat16)

    for a in range(2):
        for kind in range(3):
            head_copy(a, kind).wait_send()
    for r in range(1, n):
        swap_copy(r).wait_send()
    for kind in range(3):
        col_copy(kind).wait_send()
    pair_copy(0).wait_send()
    pair_copy(1).wait_send()
    cross_copy.wait_send()


def fused_device(inputs, out_grad, qkv_weight, out_weight, text_keys, text_values, text_mask):
    n = lax.axis_size("blk")
    rows, _, feats = inputs.shape
    depth, _, local = qkv_weight.shape
    text = text_keys.shape[0]
    heads = local // HD
    total_rows = rows * n
    length = text + total_rows
    width = depth // n
    tile = 256
    bf, f32 = jnp.bfloat16, jnp.float32
    mask = jnp.broadcast_to((text_mask == 1).astype(f32), (text, tile))
    vmem = pl.BlockSpec(memory_space=pltpu.VMEM)
    hbm = pl.BlockSpec(memory_space=pl.ANY)
    dma = pltpu.SemaphoreType.DMA
    outs = pl.pallas_call(
        functools.partial(fused_kernel, n, tile),
        out_shape=(
            jax.ShapeDtypeStruct((rows, feats), bf),
            jax.ShapeDtypeStruct((3, width, local), f32),
            jax.ShapeDtypeStruct((width, local), f32),
            jax.ShapeDtypeStruct((text // n, local), f32),
            jax.ShapeDtypeStruct((text // n, local), f32),
        ),
        in_specs=[hbm] * 4 + [vmem] * 3,
        out_specs=[vmem] * 5,
        scratch_shapes=[
            pltpu.VMEM((2, rows, depth), bf),
            pltpu.VMEM((4, depth, local), bf),
            pltpu.VMEM((4, rows, local), f32),
            pltpu.VMEM((heads, 4, total_rows, HD), bf),
            pltpu.VMEM((2, n, rows, width), bf),
            pltpu.VMEM((2, width, total_rows), bf),
            pltpu.VMEM((length, HD), bf),
            pltpu.VMEM((length, HD), bf),
            pltpu.VMEM((HD, length), bf),
            pltpu.VMEM((HD, length), bf),
            pltpu.VMEM((length, HD), f32),
            pltpu.VMEM((length, HD), f32),
            pltpu.VMEM((3, rows, local), bf),
            pltpu.VMEM((2, rows, feats), bf),
            pltpu.VMEM((2, rows, feats), bf),
            pltpu.VMEM((rows, feats), bf),
            pltpu.VMEM((rows, feats), bf),
            dma((4,)),
            dma((2, 3)),
            dma((2, 3)),
            dma((heads, n // 2, 2)),
            dma((heads, n // 2, 2)),
            dma((1,)),
            dma((n,)),
            dma((n,)),
            dma((3,)),
            dma((3,)),
            dma((3,)),
            dma((3,)),
        ],
        compiler_params=pltpu.CompilerParams(
            collective_id=0, has_side_effects=True, vmem_limit_bytes=VMEM_BYTES
        ),
        cost_estimate=pl.CostEstimate(
            flops=2 * heads * 6 * total_rows * length * HD + 16 * rows * depth * local,
            bytes_accessed=16 * depth * local,
            transcendentals=heads * total_rows * length,
        ),
    )(
        inputs.reshape(rows, feats),
        out_grad.reshape(rows, feats),
        jnp.transpose(qkv_weight, (1, 0, 2)),
        out_weight,
        text_keys.reshape(text, local),
        text_values.reshape(text, local),
        mask,
    )
    dx, dwqkv, dwout, dtk, dtv = outs
    return (
        dx.reshape(rows, 1, feats),
        jnp.transpose(dwqkv, (1, 0, 2)),
        dwout,
        dtk.reshape(text // n, 1, local),
        dtv.reshape(text // n, 1, local),
    )


def per_device(inputs, out_grad, qkv_weight, out_weight, text_keys, text_values, text_mask):
    n = lax.axis_size("blk")
    rows, seqs, _ = inputs.shape
    depth = qkv_weight.shape[0]
    fits = (
        seqs == 1
        and lax.axis_size("head") == 4
        and n % 2 == 0
        and rows % 64 == 0
        and (rows * n) % 256 == 0
        and rows * n <= 2048
        and depth % (128 * n) == 0
        and text_keys.shape[0] % (8 * n) == 0
    )
    chosen = fused_device if fits else plain_device
    return chosen(inputs, out_grad, qkv_weight, out_weight, text_keys, text_values, text_mask)


def solution(mesh):
    return jax.shard_map(
        per_device,
        mesh=mesh,
        in_specs=(
            P("blk", None, "head"),
            P("blk", None, "head"),
            P(None, None, "head"),
            P(None, "head"),
            P(None, None, "head"),
            P(None, None, "head"),
            P(),
        ),
        out_specs=(
            P("blk", None, "head"),
            P("blk", None, "head"),
            P("blk", "head"),
            P("blk", None, "head"),
            P("blk", None, "head"),
        ),
        check_vma=False,
    )
```

```python
import functools

import jax
import jax.numpy as jnp
from jax import lax
from jax.experimental import pallas as pl
from jax.experimental.pallas import tpu as pltpu
from jax.sharding import PartitionSpec as P

HD = 128


masked_fill = -1000000000.0


def masked_logits(query_heads, key_rows, valid_rows, score_scale):
    logits = (
        jnp.einsum("vsne,jsne->snvj", query_heads, key_rows, preferred_element_type=jnp.float32)
        * score_scale
    )
    if valid_rows is not None:
        logits = jnp.where(valid_rows.T[:, None, None, :], logits, masked_fill)
    return logits


def attend_block(softmax_state, query_heads, key_rows, value_rows, valid_rows, score_scale):
    running_max, running_sum, running_acc = softmax_state
    logits = masked_logits(query_heads, key_rows, valid_rows, score_scale)
    new_max = jnp.maximum(running_max, jnp.max(logits, axis=-1))
    factor = jnp.exp(running_max - new_max)
    weights = jnp.exp(logits - new_max[..., None])
    new_sum = running_sum * factor + jnp.sum(weights, axis=-1)
    update = jnp.einsum(
        "snvj,jsne->snve",
        weights.astype(jnp.bfloat16),
        value_rows,
        preferred_element_type=jnp.float32,
    )
    return (new_max, new_sum, running_acc * factor[..., None] + update)


def grad_block(
    query_heads, grad_heads, key_rows, value_rows, valid_rows, log_total, row_dot, score_scale
):
    logits = masked_logits(query_heads, key_rows, valid_rows, score_scale)
    probabilities = jnp.exp(logits - log_total[..., None])
    grad_values = jnp.einsum(
        "snvj,vsne->jsne",
        probabilities.astype(jnp.bfloat16),
        grad_heads,
        preferred_element_type=jnp.float32,
    )
    grad_probs = jnp.einsum(
        "vsne,jsne->snvj", grad_heads, value_rows, preferred_element_type=jnp.float32
    )
    grad_logits = (probabilities * (grad_probs - row_dot[..., None]) * score_scale).astype(
        jnp.bfloat16
    )
    grad_queries = jnp.einsum(
        "snvj,jsne->vsne", grad_logits, key_rows, preferred_element_type=jnp.float32
    )
    grad_keys = jnp.einsum(
        "snvj,vsne->jsne", grad_logits, query_heads, preferred_element_type=jnp.float32
    )
    return (grad_queries, jnp.stack([grad_keys, grad_values], axis=2))


def key_blocks(full_kv, shard_rows, shards, seq_count, head_count, head_dim):
    group_size = 1
    while group_size * shard_rows < 512 and group_size < shards:
        group_size = group_size * 2
    return full_kv.reshape(
        shards // group_size, group_size * shard_rows, seq_count, 2, head_count, head_dim
    )


def plain_device(inputs, out_grad, qkv_weight, out_weight, text_keys, text_values, text_mask):
    full_in, full_grad = (
        lax.all_gather(inputs, "head", axis=2, tiled=True),
        lax.all_gather(out_grad, "head", axis=2, tiled=True),
    )
    shard_rows = inputs.shape[0]
    seq_count = inputs.shape[1]
    local_width = qkv_weight.shape[2]
    head_dim = HD
    head_count = local_width // head_dim
    score_scale = head_dim ** (-0.5)
    shards = lax.axis_size("blk")
    projected = jnp.einsum(
        "vsd,dch->vsch", full_in, qkv_weight, preferred_element_type=jnp.float32
    ).astype(jnp.bfloat16)
    grad_attn = jnp.einsum(
        "vsd,dh->vsh", full_grad, out_weight, preferred_element_type=jnp.float32
    ).astype(jnp.bfloat16)
    query_heads = projected[:, :, 0].reshape(shard_rows, seq_count, head_count, head_dim)
    grad_heads = grad_attn.reshape(shard_rows, seq_count, head_count, head_dim)
    kv_local = projected[:, :, 1:]
    text_rows = text_keys.shape[0]
    valid_text = text_mask == 1
    text_key_heads = text_keys.reshape(text_rows, seq_count, head_count, head_dim)
    text_value_heads = text_values.reshape(text_rows, seq_count, head_count, head_dim)
    start_state = (
        jnp.full((seq_count, head_count, shard_rows), -1e30, jnp.float32),
        jnp.zeros((seq_count, head_count, shard_rows), jnp.float32),
        jnp.zeros((seq_count, head_count, shard_rows, head_dim), jnp.float32),
    )
    softmax_state = attend_block(
        start_state, query_heads, text_key_heads, text_value_heads, valid_text, score_scale
    )
    kv_piece = lax.all_gather(kv_local, "blk", axis=0, tiled=True)
    key_slice = kv_piece.reshape(kv_piece.shape[0], seq_count, 2, head_count, head_dim)
    softmax_state = attend_block(
        softmax_state, query_heads, key_slice[:, :, 0], key_slice[:, :, 1], None, score_scale
    )
    run_max, run_sum, run_acc = softmax_state
    out_heads = jnp.transpose(run_acc / run_sum[..., None], (2, 0, 1, 3)).astype(jnp.bfloat16)
    attn_out = out_heads.reshape(shard_rows, seq_count, local_width)
    log_total = run_max + jnp.log(run_sum)
    row_dot = jnp.transpose(
        jnp.sum(grad_heads.astype(jnp.float32) * out_heads.astype(jnp.float32), axis=-1), (1, 2, 0)
    )
    text_query_grads, text_terms = grad_block(
        query_heads,
        grad_heads,
        text_key_heads,
        text_value_heads,
        valid_text,
        log_total,
        row_dot,
        score_scale,
    )
    text_sums = lax.psum_scatter(
        text_terms.reshape(text_rows, seq_count, 2, local_width).astype(jnp.bfloat16),
        "blk",
        scatter_dimension=0,
        tiled=True,
    ).astype(jnp.float32)
    full_kv = lax.all_gather(kv_local, "blk", axis=0, tiled=True)
    blocks = key_blocks(full_kv, shard_rows, shards, seq_count, head_count, head_dim)

    def backward_step(running, kv_block):
        partial_value, key_term = grad_block(
            query_heads,
            grad_heads,
            kv_block[:, :, 0],
            kv_block[:, :, 1],
            None,
            log_total,
            row_dot,
            score_scale,
        )
        return (running + partial_value, key_term)

    query_grads, key_terms = lax.scan(backward_step, text_query_grads, blocks)
    key_terms = key_terms.reshape(full_kv.shape[0], seq_count, 2, local_width)
    kv_grads = lax.psum_scatter(
        key_terms.astype(jnp.bfloat16), "blk", scatter_dimension=0, tiled=True
    )
    grad_projected = jnp.concatenate(
        [query_grads.astype(jnp.bfloat16).reshape(shard_rows, seq_count, 1, local_width), kv_grads],
        axis=2,
    )
    input_terms = jnp.einsum(
        "vsch,dch->vsd", grad_projected, qkv_weight, preferred_element_type=jnp.float32
    )
    grad_inputs = lax.psum_scatter(
        input_terms.astype(jnp.bfloat16), "head", scatter_dimension=2, tiled=True
    )
    qkv_part = jnp.einsum(
        "vsd,vsch->dch", full_in, grad_projected, preferred_element_type=jnp.float32
    )
    out_part = jnp.einsum("vsd,vsh->dh", full_grad, attn_out, preferred_element_type=jnp.float32)
    weight_grads = lax.psum_scatter(
        jnp.concatenate([qkv_part, out_part[:, None]], axis=1).astype(jnp.bfloat16),
        "blk",
        scatter_dimension=0,
        tiled=True,
    ).astype(jnp.float32)
    return (
        grad_inputs,
        weight_grads[:, :3],
        weight_grads[:, 3],
        text_sums[:, :, 0],
        text_sums[:, :, 1],
    )


MESH = pl.DeviceIdType.MESH
LOG2E = 1.4426950408889634
VMEM_BYTES = 60 * 1024 * 1024


def dot(a, b, contract=((1,), (0,))):
    return lax.dot_general(a, b, (contract, ((), ())), preferred_element_type=jnp.float32)


def fused_kernel(
    n,
    tile,
    x_hbm,
    g_hbm,
    wqkv_hbm,
    wout_hbm,
    tk_ref,
    tv_ref,
    mask_ref,
    dx_ref,
    dwqkv_ref,
    dwout_ref,
    dtk_ref,
    dtv_ref,
    full,
    weights,
    proj,
    ring,
    cols_in,
    cols_t,
    keys,
    values,
    keys_t,
    values_t,
    grad_k,
    grad_v,
    gp,
    pair_out,
    pair_in,
    cross_out,
    cross_in,
    load_sem,
    head_send,
    head_recv,
    ring_send,
    ring_recv,
    own_sem,
    swap_send,
    swap_recv,
    col_send,
    col_recv,
    red_send,
    red_recv,
):
    rows, depth = full.shape[1], full.shape[2]
    feats = x_hbm.shape[1]
    heads = ring.shape[0]
    text = tk_ref.shape[0]
    total_rows = ring.shape[2]
    width = cols_in.shape[3]
    quarter = rows // 4
    tiles = total_rows // tile
    half = n // 2
    scale = HD ** (-0.5)

    hd = lax.axis_index("head")
    me = lax.axis_index("blk")
    sib = hd + 1 - 2 * (hd % 2)
    far = (hd + 2) % 4
    diag = (sib + 2) % 4
    odd = me % 2
    pos = (1 - odd) * (me // 2) + odd * (n - 1 - me // 2)

    def blk_at(p):
        p = p % n
        hi = p // half
        return (1 - hi) * (2 * p) + hi * (2 * (n - 1 - p) + 1)

    right, left = blk_at(pos + 1), blk_at(pos + n - 1)

    def feat(j):
        return pl.ds(pl.multiple_of(j * feats, 128), feats)

    def block(j):
        return pl.ds(pl.multiple_of(j * rows, 16), rows)

    w_loads = [
        pltpu.make_async_copy(wqkv_hbm, weights.at[pl.ds(0, 3)], load_sem.at[2]),
        pltpu.make_async_copy(wout_hbm, weights.at[3], load_sem.at[3]),
    ]
    own_loads = [
        pltpu.make_async_copy(src, full.at[a, :, feat(hd)], load_sem.at[a])
        for a, src in enumerate((x_hbm, g_hbm))
    ]
    for c in own_loads + w_loads:
        c.start()

    barrier = pltpu.get_barrier_semaphore()
    for r in range(1, n):
        pl.semaphore_signal(
            barrier, inc=1, device_id={"blk": (me + r) % n}, device_id_type=MESH
        )
    for other in (sib, far):
        pl.semaphore_signal(barrier, inc=1, device_id={"head": other}, device_id_type=MESH)
    pl.semaphore_wait(barrier, n + 1)

    def head_copy(a, kind):
        j = far if kind == 2 else hd
        ref = full.at[a, :, feat(j)]
        return pltpu.make_async_remote_copy(
            src_ref=ref,
            dst_ref=ref,
            send_sem=head_send.at[a, kind],
            recv_sem=head_recv.at[a, kind],
            device_id={"head": far if kind == 0 else sib},
            device_id_type=MESH,
        )

    own_loads[0].wait()
    head_copy(0, 0).start()
    head_copy(0, 1).start()
    own_loads[1].wait()
    head_copy(1, 1).start()

    def project(a, j, first=False):
        part = full[a, :, feat(j)]
        for c in (0, 1, 2) if a == 0 else (3,):
            term = dot(part, weights[c, feat(j), :])
            proj[c] = term if first else proj[c] + term

    def place(c):
        for h in range(heads):
            ring[h, c, block(me), :] = proj[c, :, h * HD : (h + 1) * HD].astype(jnp.bfloat16)

    def ring_copy(h, g, s, way):
        first, last = (0, 4) if h else ((0, 3), (3, 4))[g]
        if s == half:
            first, last = max(first, 2 * way), min(last, 2 * way + 2)
        if first >= last:
            return None
        p = pos - (s - 1) + n if way == 0 else pos + s - 1
        ref = ring.at[h, pl.ds(first, last - first), block(blk_at(p)), :]
        return pltpu.make_async_remote_copy(
            src_ref=ref,
            dst_ref=ref,
            send_sem=ring_send.at[h, g, s - 1, way],
            recv_sem=ring_recv.at[h, g, s - 1, way],
            device_id={"blk": right if way == 0 else left},
            device_id_type=MESH,
        )

    def hop(h, g, s):
        for way in range(2):
            if s > 1:
                ring_copy(h, g, s - 1, way).wait_recv()
            copy = ring_copy(h, g, s, way)
            if copy is not None:
                copy.start()

    def finish(h):
        for g in range(1 if h else 2):
            for way in range(2):
                for s in range(1, half + 1):
                    copy = ring_copy(h, g, s, way)
                    if copy is not None:
                        if s == half:
                            copy.wait_recv()
                        copy.wait_send()

    for c in w_loads:
        c.wait()
    project(0, hd, True)
    head_copy(0, 1).wait_recv()
    project(0, sib)
    head_copy(0, 0).wait_recv()
    head_copy(0, 2).start()
    head_copy(1, 0).start()
    project(0, far)
    head_copy(0, 2).wait_recv()
    project(0, diag)
    for c in range(3):
        place(c)
    hop(0, 0, 1)
    project(1, hd, True)
    head_copy(1, 1).wait_recv()
    project(1, sib)
    hop(0, 0, 2)
    head_copy(1, 0).wait_recv()
    head_copy(1, 2).start()
    project(1, far)
    head_copy(1, 2).wait_recv()
    project(1, diag)
    place(3)
    hop(0, 1, 1)

    mine = pl.ds(pl.multiple_of(hd * quarter, 16), quarter)

    def wide(j):
        return pl.ds(pl.multiple_of(j * width, 128), width)

    def swap_copy(r):
        to = (me + r) % n
        return pltpu.make_async_remote_copy(
            src_ref=full.at[:, mine, wide(to)],
            dst_ref=cols_in.at[:, me, mine, :],
            send_sem=swap_send.at[r],
            recv_sem=swap_recv.at[r],
            device_id={"blk": to},
            device_id_type=MESH,
        )

    own_cols = pltpu.make_async_copy(
        full.at[:, mine, wide(me)], cols_in.at[:, me, mine, :], own_sem.at[0]
    )

    def swap_start():
        own_cols.start()
        for r in range(1, n):
            swap_copy(r).start()

    def col_copy(kind):
        j = far if kind == 2 else hd
        ref = cols_in.at[:, :, pl.ds(pl.multiple_of(j * quarter, 16), quarter), :]
        return pltpu.make_async_remote_copy(
            src_ref=ref,
            dst_ref=ref,
            send_sem=col_send.at[kind],
            recv_sem=col_recv.at[kind],
            device_id={"head": far if kind == 0 else sib},
            device_id_type=MESH,
        )

    def cols_start():
        own_cols.wait()
        for r in range(1, n):
            swap_copy(r).wait_recv()
        col_copy(0).start()
        col_copy(1).start()

    def cols_forward():
        col_copy(0).wait_recv()
        col_copy(2).start()

    def attend(h, events):
        lanes = pl.ds(h * HD, HD)
        keys[pl.ds(0, text), :] = tk_ref[:, lanes]
        keys[pl.ds(text, total_rows), :] = ring[h, 1]
        values[pl.ds(0, text), :] = tv_ref[:, lanes]
        values[pl.ds(text, total_rows), :] = ring[h, 2]
        keys_t[...] = keys[...].T
        values_t[...] = values[...].T
        grad_k[...] = jnp.zeros_like(grad_k)
        grad_v[...] = jnp.zeros_like(grad_v)

        @pl.loop(0, tiles)
        def _(i):
            for at, run in events:
                pl.when(i == at)(run)
            here = pl.ds(pl.multiple_of(i * tile, tile), tile)
            q = ring[h, 0, here, :]
            go = ring[h, 3, here, :]
            go_t = go.T
            logits = dot(keys[...], q.T)
            gp_t = dot(values[...], go_t)
            logits = jnp.concatenate(
                [jnp.where(mask_ref[...] > 0.0, logits[:text], masked_fill / scale), logits[text:]],
                axis=0,
            )
            top = jnp.max(logits, axis=0, keepdims=True)
            p = jnp.exp2((logits - top) * (scale * LOG2E))
            inv = 1.0 / jnp.sum(p, axis=0, keepdims=True)
            pb = p.astype(jnp.bfloat16)
            out_t = (dot(values_t[...], pb) * inv).astype(jnp.bfloat16)
            go_f = go_t.astype(jnp.float32)
            grad_v[...] += dot(pb, (go_f * inv).astype(jnp.bfloat16).T)
            row_dot = jnp.sum(go_f * out_t.astype(jnp.float32), axis=0, keepdims=True)
            ds = (p * ((gp_t - row_dot) * (inv * scale))).astype(jnp.bfloat16)
            dq_t = dot(keys_t[...], ds)
            grad_k[...] += dot(ds, q)
            ring[h, 0, here, :] = dq_t.astype(jnp.bfloat16).T
            ring[h, 3, here, :] = out_t.T

        ring[h, 1] = grad_k[pl.ds(text, total_rows), :].astype(jnp.bfloat16)
        ring[h, 2] = grad_v[pl.ds(text, total_rows), :].astype(jnp.bfloat16)
        part = text // n
        own_text = pl.ds(pl.multiple_of(me * part, 8), part)
        dtk_ref[:, lanes] = grad_k[own_text, :]
        dtv_ref[:, lanes] = grad_v[own_text, :]

    for s in range(2, half):
        hop(0, 1, s)
        if s + 1 < half:
            hop(0, 0, s + 1)
    hop(1, 0, 1)
    hop(0, 0, half)
    hop(0, 1, half)
    for h in range(heads):
        finish(h)
        todo = []
        if h + 1 < heads:
            todo = [functools.partial(hop, h + 1, 0, s) for s in range(2, half + 1)]
        if h + 2 < heads:
            todo.insert(half - 2, functools.partial(hop, h + 2, 0, 1))
        if h == 0:
            todo.insert(0, swap_start)
        if h == 1:
            todo.insert(1, cols_start)
            todo.append(cols_forward)
        attend(h, [(e * tiles // len(todo), run) for e, run in enumerate(todo)])

    for h in range(heads):
        for c in range(3):
            gp[c, :, pl.ds(h * HD, HD)] = ring[h, c, block(me), :]

    def input_term(j):
        return sum(dot(gp[c], weights[c, feat(j), :], ((1,), (1,))) for c in range(3))

    def pair_copy(k):
        return pltpu.make_async_remote_copy(
            src_ref=pair_out.at[k],
            dst_ref=pair_in.at[k],
            send_sem=red_send.at[k],
            recv_sem=red_recv.at[k],
            device_id={"head": sib},
            device_id_type=MESH,
        )

    cross_copy = pltpu.make_async_remote_copy(
        src_ref=cross_out,
        dst_ref=cross_in,
        send_sem=red_send.at[2],
        recv_sem=red_recv.at[2],
        device_id={"head": far},
        device_id_type=MESH,
    )
    pair_out[1] = input_term(diag).astype(jnp.bfloat16)
    pair_copy(1).start()
    pair_out[0] = input_term(sib).astype(jnp.bfloat16)
    pair_copy(0).start()
    far_term = input_term(far)
    pair_copy(1).wait_recv()
    cross_out[...] = (far_term + pair_in[1].astype(jnp.float32)).astype(jnp.bfloat16)
    cross_copy.start()
    own_term = input_term(hd)
    pair_copy(0).wait_recv()
    own_term = own_term + pair_in[0].astype(jnp.float32)

    col_copy(1).wait_recv()
    col_copy(2).wait_recv()
    for a in range(2):
        cols_t[a] = cols_in[a].reshape(total_rows, width).T
    for h in range(heads):
        lanes = pl.ds(h * HD, HD)
        three = jnp.concatenate([ring[h, 0], ring[h, 1], ring[h, 2]], axis=1)
        term = dot(cols_t[0], three)
        for c in range(3):
            dwqkv_ref[c, :, lanes] = term[:, c * HD : (c + 1) * HD].astype(jnp.bfloat16)
        dwout_ref[:, lanes] = dot(cols_t[1], ring[h, 3]).astype(jnp.bfloat16)

    cross_copy.wait_recv()
    dx_ref[...] = (own_term + cross_in[...].astype(jnp.float32)).astype(jnp.bfloat16)

    for a in range(2):
        for kind in range(3):
            head_copy(a, kind).wait_send()
    for r in range(1, n):
        swap_copy(r).wait_send()
    for kind in range(3):
        col_copy(kind).wait_send()
    pair_copy(0).wait_send()
    pair_copy(1).wait_send()
    cross_copy.wait_send()


def fused_device(inputs, out_grad, qkv_weight, out_weight, text_keys, text_values, text_mask):
    n = lax.axis_size("blk")
    rows, _, feats = inputs.shape
    depth, _, local = qkv_weight.shape
    text = text_keys.shape[0]
    heads = local // HD
    total_rows = rows * n
    length = text + total_rows
    width = depth // n
    tile = 256
    bf, f32 = jnp.bfloat16, jnp.float32
    mask = jnp.broadcast_to((text_mask == 1).astype(f32), (text, tile))
    vmem = pl.BlockSpec(memory_space=pltpu.VMEM)
    hbm = pl.BlockSpec(memory_space=pl.ANY)
    dma = pltpu.SemaphoreType.DMA
    outs = pl.pallas_call(
        functools.partial(fused_kernel, n, tile),
        out_shape=(
            jax.ShapeDtypeStruct((rows, feats), bf),
            jax.ShapeDtypeStruct((3, width, local), bf),
            jax.ShapeDtypeStruct((width, local), bf),
            jax.ShapeDtypeStruct((text // n, local), f32),
            jax.ShapeDtypeStruct((text // n, local), f32),
        ),
        in_specs=[hbm] * 4 + [vmem] * 3,
        out_specs=[vmem] * 5,
        scratch_shapes=[
            pltpu.VMEM((2, rows, depth), bf),
            pltpu.VMEM((4, depth, local), bf),
            pltpu.VMEM((4, rows, local), f32),
            pltpu.VMEM((heads, 4, total_rows, HD), bf),
            pltpu.VMEM((2, n, rows, width), bf),
            pltpu.VMEM((2, width, total_rows), bf),
            pltpu.VMEM((length, HD), bf),
            pltpu.VMEM((length, HD), bf),
            pltpu.VMEM((HD, length), bf),
            pltpu.VMEM((HD, length), bf),
            pltpu.VMEM((length, HD), f32),
            pltpu.VMEM((length, HD), f32),
            pltpu.VMEM((3, rows, local), bf),
            pltpu.VMEM((2, rows, feats), bf),
            pltpu.VMEM((2, rows, feats), bf),
            pltpu.VMEM((rows, feats), bf),
            pltpu.VMEM((rows, feats), bf),
            dma((4,)),
            dma((2, 3)),
            dma((2, 3)),
            dma((heads, 2, n // 2, 2)),
            dma((heads, 2, n // 2, 2)),
            dma((1,)),
            dma((n,)),
            dma((n,)),
            dma((3,)),
            dma((3,)),
            dma((3,)),
            dma((3,)),
        ],
        compiler_params=pltpu.CompilerParams(
            collective_id=0, has_side_effects=True, vmem_limit_bytes=VMEM_BYTES
        ),
        cost_estimate=pl.CostEstimate(
            flops=2 * heads * 6 * total_rows * length * HD + 16 * rows * depth * local,
            bytes_accessed=16 * depth * local,
            transcendentals=heads * total_rows * length,
        ),
    )(
        inputs.reshape(rows, feats),
        out_grad.reshape(rows, feats),
        jnp.transpose(qkv_weight, (1, 0, 2)),
        out_weight,
        text_keys.reshape(text, local),
        text_values.reshape(text, local),
        mask,
    )
    dx, dwqkv, dwout, dtk, dtv = outs
    return (
        dx.reshape(rows, 1, feats),
        jnp.transpose(dwqkv, (1, 0, 2)).astype(f32),
        dwout.astype(f32),
        dtk.reshape(text // n, 1, local),
        dtv.reshape(text // n, 1, local),
    )


def per_device(inputs, out_grad, qkv_weight, out_weight, text_keys, text_values, text_mask):
    n = lax.axis_size("blk")
    rows, seqs, _ = inputs.shape
    depth = qkv_weight.shape[0]
    fits = (
        seqs == 1
        and lax.axis_size("head") == 4
        and n % 2 == 0
        and rows % 64 == 0
        and (rows * n) % 256 == 0
        and rows * n <= 2048
        and depth % (128 * n) == 0
        and text_keys.shape[0] % (8 * n) == 0
    )
    chosen = fused_device if fits else plain_device
    return chosen(inputs, out_grad, qkv_weight, out_weight, text_keys, text_values, text_mask)


def solution(mesh):
    return jax.shard_map(
        per_device,
        mesh=mesh,
        in_specs=(
            P("blk", None, "head"),
            P("blk", None, "head"),
            P(None, None, "head"),
            P(None, "head"),
            P(None, None, "head"),
            P(None, None, "head"),
            P(),
        ),
        out_specs=(
            P("blk", None, "head"),
            P("blk", None, "head"),
            P("blk", "head"),
            P("blk", None, "head"),
            P("blk", None, "head"),
        ),
        check_vma=False,
    )
```

```python
import functools

import jax
import jax.numpy as jnp
from jax import lax
from jax.experimental import pallas as pl
from jax.experimental.pallas import tpu as pltpu
from jax.sharding import PartitionSpec as P

HD = 128


masked_fill = -1000000000.0


def masked_logits(query_heads, key_rows, valid_rows, score_scale):
    logits = (
        jnp.einsum("vsne,jsne->snvj", query_heads, key_rows, preferred_element_type=jnp.float32)
        * score_scale
    )
    if valid_rows is not None:
        logits = jnp.where(valid_rows.T[:, None, None, :], logits, masked_fill)
    return logits


def attend_block(softmax_state, query_heads, key_rows, value_rows, valid_rows, score_scale):
    running_max, running_sum, running_acc = softmax_state
    logits = masked_logits(query_heads, key_rows, valid_rows, score_scale)
    new_max = jnp.maximum(running_max, jnp.max(logits, axis=-1))
    factor = jnp.exp(running_max - new_max)
    weights = jnp.exp(logits - new_max[..., None])
    new_sum = running_sum * factor + jnp.sum(weights, axis=-1)
    update = jnp.einsum(
        "snvj,jsne->snve",
        weights.astype(jnp.bfloat16),
        value_rows,
        preferred_element_type=jnp.float32,
    )
    return (new_max, new_sum, running_acc * factor[..., None] + update)


def grad_block(
    query_heads, grad_heads, key_rows, value_rows, valid_rows, log_total, row_dot, score_scale
):
    logits = masked_logits(query_heads, key_rows, valid_rows, score_scale)
    probabilities = jnp.exp(logits - log_total[..., None])
    grad_values = jnp.einsum(
        "snvj,vsne->jsne",
        probabilities.astype(jnp.bfloat16),
        grad_heads,
        preferred_element_type=jnp.float32,
    )
    grad_probs = jnp.einsum(
        "vsne,jsne->snvj", grad_heads, value_rows, preferred_element_type=jnp.float32
    )
    grad_logits = (probabilities * (grad_probs - row_dot[..., None]) * score_scale).astype(
        jnp.bfloat16
    )
    grad_queries = jnp.einsum(
        "snvj,jsne->vsne", grad_logits, key_rows, preferred_element_type=jnp.float32
    )
    grad_keys = jnp.einsum(
        "snvj,vsne->jsne", grad_logits, query_heads, preferred_element_type=jnp.float32
    )
    return (grad_queries, jnp.stack([grad_keys, grad_values], axis=2))


def key_blocks(full_kv, shard_rows, shards, seq_count, head_count, head_dim):
    group_size = 1
    while group_size * shard_rows < 512 and group_size < shards:
        group_size = group_size * 2
    return full_kv.reshape(
        shards // group_size, group_size * shard_rows, seq_count, 2, head_count, head_dim
    )


def plain_device(inputs, out_grad, qkv_weight, out_weight, text_keys, text_values, text_mask):
    full_in, full_grad = (
        lax.all_gather(inputs, "head", axis=2, tiled=True),
        lax.all_gather(out_grad, "head", axis=2, tiled=True),
    )
    shard_rows = inputs.shape[0]
    seq_count = inputs.shape[1]
    local_width = qkv_weight.shape[2]
    head_dim = HD
    head_count = local_width // head_dim
    score_scale = head_dim ** (-0.5)
    shards = lax.axis_size("blk")
    projected = jnp.einsum(
        "vsd,dch->vsch", full_in, qkv_weight, preferred_element_type=jnp.float32
    ).astype(jnp.bfloat16)
    grad_attn = jnp.einsum(
        "vsd,dh->vsh", full_grad, out_weight, preferred_element_type=jnp.float32
    ).astype(jnp.bfloat16)
    query_heads = projected[:, :, 0].reshape(shard_rows, seq_count, head_count, head_dim)
    grad_heads = grad_attn.reshape(shard_rows, seq_count, head_count, head_dim)
    kv_local = projected[:, :, 1:]
    text_rows = text_keys.shape[0]
    valid_text = text_mask == 1
    text_key_heads = text_keys.reshape(text_rows, seq_count, head_count, head_dim)
    text_value_heads = text_values.reshape(text_rows, seq_count, head_count, head_dim)
    start_state = (
        jnp.full((seq_count, head_count, shard_rows), -1e30, jnp.float32),
        jnp.zeros((seq_count, head_count, shard_rows), jnp.float32),
        jnp.zeros((seq_count, head_count, shard_rows, head_dim), jnp.float32),
    )
    softmax_state = attend_block(
        start_state, query_heads, text_key_heads, text_value_heads, valid_text, score_scale
    )
    kv_piece = lax.all_gather(kv_local, "blk", axis=0, tiled=True)
    key_slice = kv_piece.reshape(kv_piece.shape[0], seq_count, 2, head_count, head_dim)
    softmax_state = attend_block(
        softmax_state, query_heads, key_slice[:, :, 0], key_slice[:, :, 1], None, score_scale
    )
    run_max, run_sum, run_acc = softmax_state
    out_heads = jnp.transpose(run_acc / run_sum[..., None], (2, 0, 1, 3)).astype(jnp.bfloat16)
    attn_out = out_heads.reshape(shard_rows, seq_count, local_width)
    log_total = run_max + jnp.log(run_sum)
    row_dot = jnp.transpose(
        jnp.sum(grad_heads.astype(jnp.float32) * out_heads.astype(jnp.float32), axis=-1), (1, 2, 0)
    )
    text_query_grads, text_terms = grad_block(
        query_heads,
        grad_heads,
        text_key_heads,
        text_value_heads,
        valid_text,
        log_total,
        row_dot,
        score_scale,
    )
    text_sums = lax.psum_scatter(
        text_terms.reshape(text_rows, seq_count, 2, local_width).astype(jnp.bfloat16),
        "blk",
        scatter_dimension=0,
        tiled=True,
    ).astype(jnp.float32)
    full_kv = lax.all_gather(kv_local, "blk", axis=0, tiled=True)
    blocks = key_blocks(full_kv, shard_rows, shards, seq_count, head_count, head_dim)

    def backward_step(running, kv_block):
        partial_value, key_term = grad_block(
            query_heads,
            grad_heads,
            kv_block[:, :, 0],
            kv_block[:, :, 1],
            None,
            log_total,
            row_dot,
            score_scale,
        )
        return (running + partial_value, key_term)

    query_grads, key_terms = lax.scan(backward_step, text_query_grads, blocks)
    key_terms = key_terms.reshape(full_kv.shape[0], seq_count, 2, local_width)
    kv_grads = lax.psum_scatter(
        key_terms.astype(jnp.bfloat16), "blk", scatter_dimension=0, tiled=True
    )
    grad_projected = jnp.concatenate(
        [query_grads.astype(jnp.bfloat16).reshape(shard_rows, seq_count, 1, local_width), kv_grads],
        axis=2,
    )
    input_terms = jnp.einsum(
        "vsch,dch->vsd", grad_projected, qkv_weight, preferred_element_type=jnp.float32
    )
    grad_inputs = lax.psum_scatter(
        input_terms.astype(jnp.bfloat16), "head", scatter_dimension=2, tiled=True
    )
    qkv_part = jnp.einsum(
        "vsd,vsch->dch", full_in, grad_projected, preferred_element_type=jnp.float32
    )
    out_part = jnp.einsum("vsd,vsh->dh", full_grad, attn_out, preferred_element_type=jnp.float32)
    weight_grads = lax.psum_scatter(
        jnp.concatenate([qkv_part, out_part[:, None]], axis=1).astype(jnp.bfloat16),
        "blk",
        scatter_dimension=0,
        tiled=True,
    ).astype(jnp.float32)
    return (
        grad_inputs,
        weight_grads[:, :3],
        weight_grads[:, 3],
        text_sums[:, :, 0],
        text_sums[:, :, 1],
    )


MESH = pl.DeviceIdType.MESH
LOG2E = 1.4426950408889634
VMEM_BYTES = 60 * 1024 * 1024


def dot(a, b, contract=((1,), (0,))):
    return lax.dot_general(a, b, (contract, ((), ())), preferred_element_type=jnp.float32)


def fused_kernel(
    n,
    tile,
    x_hbm,
    g_hbm,
    wqkv_hbm,
    wout_hbm,
    tk_ref,
    tv_ref,
    mask_ref,
    dx_ref,
    dwqkv_ref,
    dwout_ref,
    dtk_ref,
    dtv_ref,
    full,
    weights,
    proj,
    ring,
    cols_in,
    cols_t,
    keys,
    values,
    keys_t,
    values_t,
    grad_k,
    grad_v,
    gp,
    pair_out,
    pair_in,
    cross_out,
    cross_in,
    load_sem,
    head_send,
    head_recv,
    ring_send,
    ring_recv,
    own_sem,
    swap_send,
    swap_recv,
    col_send,
    col_recv,
    red_send,
    red_recv,
):
    rows, depth = full.shape[1], full.shape[2]
    feats = x_hbm.shape[1]
    heads = ring.shape[0]
    text = tk_ref.shape[0]
    total_rows = ring.shape[2]
    width = cols_in.shape[3]
    quarter = rows // 4
    tiles = total_rows // tile
    half = n // 2
    scale = HD ** (-0.5)
    chunk = 512
    chunks = [(0, text)] + [(text + k * chunk, chunk) for k in range(total_rows // chunk)]

    hd = lax.axis_index("head")
    me = lax.axis_index("blk")
    sib = hd + 1 - 2 * (hd % 2)
    far = (hd + 2) % 4
    diag = (sib + 2) % 4
    odd = me % 2
    pos = (1 - odd) * (me // 2) + odd * (n - 1 - me // 2)

    def blk_at(p):
        p = p % n
        hi = p // half
        return (1 - hi) * (2 * p) + hi * (2 * (n - 1 - p) + 1)

    right, left = blk_at(pos + 1), blk_at(pos + n - 1)

    def feat(j):
        return pl.ds(pl.multiple_of(j * feats, 128), feats)

    def block(j):
        return pl.ds(pl.multiple_of(j * rows, 16), rows)

    w_loads = [
        pltpu.make_async_copy(wqkv_hbm, weights.at[pl.ds(0, 3)], load_sem.at[2]),
        pltpu.make_async_copy(wout_hbm, weights.at[3], load_sem.at[3]),
    ]
    own_loads = [
        pltpu.make_async_copy(src, full.at[a, :, feat(hd)], load_sem.at[a])
        for a, src in enumerate((x_hbm, g_hbm))
    ]
    for c in own_loads + w_loads:
        c.start()

    barrier = pltpu.get_barrier_semaphore()
    for r in range(1, n):
        pl.semaphore_signal(
            barrier, inc=1, device_id={"blk": (me + r) % n}, device_id_type=MESH
        )
    for other in (sib, far):
        pl.semaphore_signal(barrier, inc=1, device_id={"head": other}, device_id_type=MESH)
    pl.semaphore_wait(barrier, n + 1)

    def head_copy(a, kind):
        j = far if kind == 2 else hd
        ref = full.at[a, :, feat(j)]
        return pltpu.make_async_remote_copy(
            src_ref=ref,
            dst_ref=ref,
            send_sem=head_send.at[a, kind],
            recv_sem=head_recv.at[a, kind],
            device_id={"head": far if kind == 0 else sib},
            device_id_type=MESH,
        )

    own_loads[0].wait()
    head_copy(0, 0).start()
    head_copy(0, 1).start()
    own_loads[1].wait()
    head_copy(1, 1).start()

    def project(a, j, first=False):
        part = full[a, :, feat(j)]
        for c in (0, 1, 2) if a == 0 else (3,):
            term = dot(part, weights[c, feat(j), :])
            proj[c] = term if first else proj[c] + term

    def place(c):
        for h in range(heads):
            ring[h, c, block(me), :] = proj[c, :, h * HD : (h + 1) * HD].astype(jnp.bfloat16)

    def ring_copy(h, g, s, way):
        first, last = (0, 4) if h else ((0, 3), (3, 4))[g]
        if s == half:
            first, last = max(first, 2 * way), min(last, 2 * way + 2)
        if first >= last:
            return None
        p = pos - (s - 1) + n if way == 0 else pos + s - 1
        ref = ring.at[h, pl.ds(first, last - first), block(blk_at(p)), :]
        return pltpu.make_async_remote_copy(
            src_ref=ref,
            dst_ref=ref,
            send_sem=ring_send.at[h, g, s - 1, way],
            recv_sem=ring_recv.at[h, g, s - 1, way],
            device_id={"blk": right if way == 0 else left},
            device_id_type=MESH,
        )

    def hop(h, g, s):
        for way in range(2):
            if s > 1:
                ring_copy(h, g, s - 1, way).wait_recv()
            copy = ring_copy(h, g, s, way)
            if copy is not None:
                copy.start()

    def finish(h):
        for g in range(1 if h else 2):
            for way in range(2):
                for s in range(1, half + 1):
                    copy = ring_copy(h, g, s, way)
                    if copy is not None:
                        if s == half:
                            copy.wait_recv()
                        copy.wait_send()

    for c in w_loads:
        c.wait()
    project(0, hd, True)
    head_copy(0, 1).wait_recv()
    project(0, sib)
    head_copy(0, 0).wait_recv()
    head_copy(0, 2).start()
    head_copy(1, 0).start()
    project(0, far)
    head_copy(0, 2).wait_recv()
    project(0, diag)
    for c in range(3):
        place(c)
    hop(0, 0, 1)
    project(1, hd, True)
    head_copy(1, 1).wait_recv()
    project(1, sib)
    hop(0, 0, 2)
    head_copy(1, 0).wait_recv()
    head_copy(1, 2).start()
    project(1, far)
    head_copy(1, 2).wait_recv()
    project(1, diag)
    place(3)
    hop(0, 1, 1)

    mine = pl.ds(pl.multiple_of(hd * quarter, 16), quarter)

    def wide(j):
        return pl.ds(pl.multiple_of(j * width, 128), width)

    def swap_copy(r):
        to = (me + r) % n
        return pltpu.make_async_remote_copy(
            src_ref=full.at[:, mine, wide(to)],
            dst_ref=cols_in.at[:, me, mine, :],
            send_sem=swap_send.at[r],
            recv_sem=swap_recv.at[r],
            device_id={"blk": to},
            device_id_type=MESH,
        )

    own_cols = pltpu.make_async_copy(
        full.at[:, mine, wide(me)], cols_in.at[:, me, mine, :], own_sem.at[0]
    )

    def swap_start():
        own_cols.start()
        for r in range(1, n):
            swap_copy(r).start()

    def col_copy(kind):
        j = far if kind == 2 else hd
        ref = cols_in.at[:, :, pl.ds(pl.multiple_of(j * quarter, 16), quarter), :]
        return pltpu.make_async_remote_copy(
            src_ref=ref,
            dst_ref=ref,
            send_sem=col_send.at[kind],
            recv_sem=col_recv.at[kind],
            device_id={"head": far if kind == 0 else sib},
            device_id_type=MESH,
        )

    def cols_start():
        own_cols.wait()
        for r in range(1, n):
            swap_copy(r).wait_recv()
        col_copy(0).start()
        col_copy(1).start()

    def cols_forward():
        col_copy(0).wait_recv()
        col_copy(2).start()

    def attend(h, events):
        lanes = pl.ds(h * HD, HD)
        keys[pl.ds(0, text), :] = tk_ref[:, lanes]
        keys[pl.ds(text, total_rows), :] = ring[h, 1]
        values[pl.ds(0, text), :] = tv_ref[:, lanes]
        values[pl.ds(text, total_rows), :] = ring[h, 2]
        keys_t[...] = keys[...].T
        values_t[...] = values[...].T
        grad_k[...] = jnp.zeros_like(grad_k)
        grad_v[...] = jnp.zeros_like(grad_v)

        @pl.loop(0, tiles)
        def _(i):
            for at, run in events:
                pl.when(i == at)(run)
            here = pl.ds(pl.multiple_of(i * tile, tile), tile)
            q = ring[h, 0, here, :]
            go = ring[h, 3, here, :]
            q_t = q.T
            go_t = go.T
            logits = []
            top = None
            for c, (first, size) in enumerate(chunks):
                part = dot(keys[pl.ds(first, size), :], q_t)
                if c == 0:
                    part = jnp.where(mask_ref[...] > 0.0, part, masked_fill / scale)
                high = jnp.max(part, axis=0, keepdims=True)
                top = high if c == 0 else jnp.maximum(top, high)
                logits.append(part)
            top = top * (scale * LOG2E)
            weights_b = []
            total = out_t = 0.0
            for (first, size), part in zip(chunks, logits):
                p = jnp.exp2(part * (scale * LOG2E) - top)
                total = total + jnp.sum(p, axis=0, keepdims=True)
                pb = p.astype(jnp.bfloat16)
                out_t = out_t + dot(values_t[:, pl.ds(first, size)], pb)
                weights_b.append(pb)
            inv = 1.0 / total
            out_t = (out_t * inv).astype(jnp.bfloat16)
            go_s = (go_t.astype(jnp.float32) * inv).astype(jnp.bfloat16)
            row_dot = jnp.sum(
                go_s.astype(jnp.float32) * out_t.astype(jnp.float32), axis=0, keepdims=True
            )
            go_r = go_s.T

            def probs_grad(c):
                first, size = chunks[c]
                return dot(values[pl.ds(first, size), :], go_s)

            dq_t = 0.0
            ahead = probs_grad(0)
            for c, (first, size) in enumerate(chunks):
                here_k = pl.ds(first, size)
                gp_c = ahead
                if c + 1 < len(chunks):
                    ahead = probs_grad(c + 1)
                grad_v[here_k, :] += dot(weights_b[c], go_r)
                ds = weights_b[c] * (gp_c - row_dot).astype(jnp.bfloat16)
                grad_k[here_k, :] += dot(ds, q)
                dq_t = dq_t + dot(keys_t[:, here_k], ds)
            ring[h, 0, here, :] = (dq_t * scale).astype(jnp.bfloat16).T
            ring[h, 3, here, :] = out_t.T

        grad_k[...] = grad_k[...] * scale
        ring[h, 1] = grad_k[pl.ds(text, total_rows), :].astype(jnp.bfloat16)
        ring[h, 2] = grad_v[pl.ds(text, total_rows), :].astype(jnp.bfloat16)
        part = text // n
        own_text = pl.ds(pl.multiple_of(me * part, 8), part)
        dtk_ref[:, lanes] = grad_k[own_text, :]
        dtv_ref[:, lanes] = grad_v[own_text, :]

    for s in range(2, half):
        hop(0, 1, s)
        if s + 1 < half:
            hop(0, 0, s + 1)
    hop(1, 0, 1)
    hop(0, 0, half)
    hop(0, 1, half)
    for h in range(heads):
        finish(h)
        todo = []
        if h + 1 < heads:
            todo = [functools.partial(hop, h + 1, 0, s) for s in range(2, half + 1)]
        if h + 2 < heads:
            todo.insert(half - 2, functools.partial(hop, h + 2, 0, 1))
        if h == 0:
            todo.insert(0, swap_start)
        if h == 1:
            todo.insert(1, cols_start)
            todo.append(cols_forward)
        attend(h, [(e * tiles // len(todo), run) for e, run in enumerate(todo)])

    for h in range(heads):
        for c in range(3):
            gp[c, :, pl.ds(h * HD, HD)] = ring[h, c, block(me), :]

    def input_term(j):
        return sum(dot(gp[c], weights[c, feat(j), :], ((1,), (1,))) for c in range(3))

    def pair_copy(k):
        return pltpu.make_async_remote_copy(
            src_ref=pair_out.at[k],
            dst_ref=pair_in.at[k],
            send_sem=red_send.at[k],
            recv_sem=red_recv.at[k],
            device_id={"head": sib},
            device_id_type=MESH,
        )

    cross_copy = pltpu.make_async_remote_copy(
        src_ref=cross_out,
        dst_ref=cross_in,
        send_sem=red_send.at[2],
        recv_sem=red_recv.at[2],
        device_id={"head": far},
        device_id_type=MESH,
    )
    pair_out[1] = input_term(diag).astype(jnp.bfloat16)
    pair_copy(1).start()
    pair_out[0] = input_term(sib).astype(jnp.bfloat16)
    pair_copy(0).start()
    far_term = input_term(far)
    pair_copy(1).wait_recv()
    cross_out[...] = (far_term + pair_in[1].astype(jnp.float32)).astype(jnp.bfloat16)
    cross_copy.start()
    own_term = input_term(hd)
    pair_copy(0).wait_recv()
    own_term = own_term + pair_in[0].astype(jnp.float32)

    col_copy(1).wait_recv()
    col_copy(2).wait_recv()
    for a in range(2):
        cols_t[a] = cols_in[a].reshape(total_rows, width).T
    for h in range(heads):
        lanes = pl.ds(h * HD, HD)
        three = jnp.concatenate([ring[h, 0], ring[h, 1], ring[h, 2]], axis=1)
        term = dot(cols_t[0], three)
        for c in range(3):
            dwqkv_ref[c, :, lanes] = term[:, c * HD : (c + 1) * HD].astype(jnp.bfloat16)
        dwout_ref[:, lanes] = dot(cols_t[1], ring[h, 3]).astype(jnp.bfloat16)

    cross_copy.wait_recv()
    dx_ref[...] = (own_term + cross_in[...].astype(jnp.float32)).astype(jnp.bfloat16)

    for a in range(2):
        for kind in range(3):
            head_copy(a, kind).wait_send()
    for r in range(1, n):
        swap_copy(r).wait_send()
    for kind in range(3):
        col_copy(kind).wait_send()
    pair_copy(0).wait_send()
    pair_copy(1).wait_send()
    cross_copy.wait_send()


def fused_device(inputs, out_grad, qkv_weight, out_weight, text_keys, text_values, text_mask):
    n = lax.axis_size("blk")
    rows, _, feats = inputs.shape
    depth, _, local = qkv_weight.shape
    text = text_keys.shape[0]
    heads = local // HD
    total_rows = rows * n
    length = text + total_rows
    width = depth // n
    tile = 256
    bf, f32 = jnp.bfloat16, jnp.float32
    mask = jnp.broadcast_to((text_mask == 1).astype(f32), (text, tile))
    vmem = pl.BlockSpec(memory_space=pltpu.VMEM)
    hbm = pl.BlockSpec(memory_space=pl.ANY)
    dma = pltpu.SemaphoreType.DMA
    outs = pl.pallas_call(
        functools.partial(fused_kernel, n, tile),
        out_shape=(
            jax.ShapeDtypeStruct((rows, feats), bf),
            jax.ShapeDtypeStruct((3, width, local), bf),
            jax.ShapeDtypeStruct((width, local), bf),
            jax.ShapeDtypeStruct((text // n, local), f32),
            jax.ShapeDtypeStruct((text // n, local), f32),
        ),
        in_specs=[hbm] * 4 + [vmem] * 3,
        out_specs=[vmem] * 5,
        scratch_shapes=[
            pltpu.VMEM((2, rows, depth), bf),
            pltpu.VMEM((4, depth, local), bf),
            pltpu.VMEM((4, rows, local), f32),
            pltpu.VMEM((heads, 4, total_rows, HD), bf),
            pltpu.VMEM((2, n, rows, width), bf),
            pltpu.VMEM((2, width, total_rows), bf),
            pltpu.VMEM((length, HD), bf),
            pltpu.VMEM((length, HD), bf),
            pltpu.VMEM((HD, length), bf),
            pltpu.VMEM((HD, length), bf),
            pltpu.VMEM((length, HD), f32),
            pltpu.VMEM((length, HD), f32),
            pltpu.VMEM((3, rows, local), bf),
            pltpu.VMEM((2, rows, feats), bf),
            pltpu.VMEM((2, rows, feats), bf),
            pltpu.VMEM((rows, feats), bf),
            pltpu.VMEM((rows, feats), bf),
            dma((4,)),
            dma((2, 3)),
            dma((2, 3)),
            dma((heads, 2, n // 2, 2)),
            dma((heads, 2, n // 2, 2)),
            dma((1,)),
            dma((n,)),
            dma((n,)),
            dma((3,)),
            dma((3,)),
            dma((3,)),
            dma((3,)),
        ],
        compiler_params=pltpu.CompilerParams(
            collective_id=0, has_side_effects=True, vmem_limit_bytes=VMEM_BYTES
        ),
        cost_estimate=pl.CostEstimate(
            flops=2 * heads * 6 * total_rows * length * HD + 16 * rows * depth * local,
            bytes_accessed=16 * depth * local,
            transcendentals=heads * total_rows * length,
        ),
    )(
        inputs.reshape(rows, feats),
        out_grad.reshape(rows, feats),
        jnp.transpose(qkv_weight, (1, 0, 2)),
        out_weight,
        text_keys.reshape(text, local),
        text_values.reshape(text, local),
        mask,
    )
    dx, dwqkv, dwout, dtk, dtv = outs
    return (
        dx.reshape(rows, 1, feats),
        jnp.transpose(dwqkv, (1, 0, 2)).astype(f32),
        dwout.astype(f32),
        dtk.reshape(text // n, 1, local),
        dtv.reshape(text // n, 1, local),
    )


def per_device(inputs, out_grad, qkv_weight, out_weight, text_keys, text_values, text_mask):
    n = lax.axis_size("blk")
    rows, seqs, _ = inputs.shape
    depth = qkv_weight.shape[0]
    fits = (
        seqs == 1
        and lax.axis_size("head") == 4
        and n % 2 == 0
        and rows % 64 == 0
        and (rows * n) % 512 == 0
        and rows * n <= 2048
        and depth % (128 * n) == 0
        and text_keys.shape[0] % (8 * n) == 0
    )
    chosen = fused_device if fits else plain_device
    return chosen(inputs, out_grad, qkv_weight, out_weight, text_keys, text_values, text_mask)


def solution(mesh):
    return jax.shard_map(
        per_device,
        mesh=mesh,
        in_specs=(
            P("blk", None, "head"),
            P("blk", None, "head"),
            P(None, None, "head"),
            P(None, "head"),
            P(None, None, "head"),
            P(None, None, "head"),
            P(),
        ),
        out_specs=(
            P("blk", None, "head"),
            P("blk", None, "head"),
            P("blk", "head"),
            P("blk", None, "head"),
            P("blk", None, "head"),
        ),
        check_vma=False,
    )
```

```python
import functools

import jax
import jax.numpy as jnp
from jax import lax
from jax.experimental import pallas as pl
from jax.experimental.pallas import tpu as pltpu
from jax.sharding import PartitionSpec as P

HD = 128


masked_fill = -1000000000.0


def masked_logits(query_heads, key_rows, valid_rows, score_scale):
    logits = (
        jnp.einsum("vsne,jsne->snvj", query_heads, key_rows, preferred_element_type=jnp.float32)
        * score_scale
    )
    if valid_rows is not None:
        logits = jnp.where(valid_rows.T[:, None, None, :], logits, masked_fill)
    return logits


def attend_block(softmax_state, query_heads, key_rows, value_rows, valid_rows, score_scale):
    running_max, running_sum, running_acc = softmax_state
    logits = masked_logits(query_heads, key_rows, valid_rows, score_scale)
    new_max = jnp.maximum(running_max, jnp.max(logits, axis=-1))
    factor = jnp.exp(running_max - new_max)
    weights = jnp.exp(logits - new_max[..., None])
    new_sum = running_sum * factor + jnp.sum(weights, axis=-1)
    update = jnp.einsum(
        "snvj,jsne->snve",
        weights.astype(jnp.bfloat16),
        value_rows,
        preferred_element_type=jnp.float32,
    )
    return (new_max, new_sum, running_acc * factor[..., None] + update)


def grad_block(
    query_heads, grad_heads, key_rows, value_rows, valid_rows, log_total, row_dot, score_scale
):
    logits = masked_logits(query_heads, key_rows, valid_rows, score_scale)
    probabilities = jnp.exp(logits - log_total[..., None])
    grad_values = jnp.einsum(
        "snvj,vsne->jsne",
        probabilities.astype(jnp.bfloat16),
        grad_heads,
        preferred_element_type=jnp.float32,
    )
    grad_probs = jnp.einsum(
        "vsne,jsne->snvj", grad_heads, value_rows, preferred_element_type=jnp.float32
    )
    grad_logits = (probabilities * (grad_probs - row_dot[..., None]) * score_scale).astype(
        jnp.bfloat16
    )
    grad_queries = jnp.einsum(
        "snvj,jsne->vsne", grad_logits, key_rows, preferred_element_type=jnp.float32
    )
    grad_keys = jnp.einsum(
        "snvj,vsne->jsne", grad_logits, query_heads, preferred_element_type=jnp.float32
    )
    return (grad_queries, jnp.stack([grad_keys, grad_values], axis=2))


def key_blocks(full_kv, shard_rows, shards, seq_count, head_count, head_dim):
    group_size = 1
    while group_size * shard_rows < 512 and group_size < shards:
        group_size = group_size * 2
    return full_kv.reshape(
        shards // group_size, group_size * shard_rows, seq_count, 2, head_count, head_dim
    )


def plain_device(inputs, out_grad, qkv_weight, out_weight, text_keys, text_values, text_mask):
    full_in, full_grad = (
        lax.all_gather(inputs, "head", axis=2, tiled=True),
        lax.all_gather(out_grad, "head", axis=2, tiled=True),
    )
    shard_rows = inputs.shape[0]
    seq_count = inputs.shape[1]
    local_width = qkv_weight.shape[2]
    head_dim = HD
    head_count = local_width // head_dim
    score_scale = head_dim ** (-0.5)
    shards = lax.axis_size("blk")
    projected = jnp.einsum(
        "vsd,dch->vsch", full_in, qkv_weight, preferred_element_type=jnp.float32
    ).astype(jnp.bfloat16)
    grad_attn = jnp.einsum(
        "vsd,dh->vsh", full_grad, out_weight, preferred_element_type=jnp.float32
    ).astype(jnp.bfloat16)
    query_heads = projected[:, :, 0].reshape(shard_rows, seq_count, head_count, head_dim)
    grad_heads = grad_attn.reshape(shard_rows, seq_count, head_count, head_dim)
    kv_local = projected[:, :, 1:]
    text_rows = text_keys.shape[0]
    valid_text = text_mask == 1
    text_key_heads = text_keys.reshape(text_rows, seq_count, head_count, head_dim)
    text_value_heads = text_values.reshape(text_rows, seq_count, head_count, head_dim)
    start_state = (
        jnp.full((seq_count, head_count, shard_rows), -1e30, jnp.float32),
        jnp.zeros((seq_count, head_count, shard_rows), jnp.float32),
        jnp.zeros((seq_count, head_count, shard_rows, head_dim), jnp.float32),
    )
    softmax_state = attend_block(
        start_state, query_heads, text_key_heads, text_value_heads, valid_text, score_scale
    )
    kv_piece = lax.all_gather(kv_local, "blk", axis=0, tiled=True)
    key_slice = kv_piece.reshape(kv_piece.shape[0], seq_count, 2, head_count, head_dim)
    softmax_state = attend_block(
        softmax_state, query_heads, key_slice[:, :, 0], key_slice[:, :, 1], None, score_scale
    )
    run_max, run_sum, run_acc = softmax_state
    out_heads = jnp.transpose(run_acc / run_sum[..., None], (2, 0, 1, 3)).astype(jnp.bfloat16)
    attn_out = out_heads.reshape(shard_rows, seq_count, local_width)
    log_total = run_max + jnp.log(run_sum)
    row_dot = jnp.transpose(
        jnp.sum(grad_heads.astype(jnp.float32) * out_heads.astype(jnp.float32), axis=-1), (1, 2, 0)
    )
    text_query_grads, text_terms = grad_block(
        query_heads,
        grad_heads,
        text_key_heads,
        text_value_heads,
        valid_text,
        log_total,
        row_dot,
        score_scale,
    )
    text_sums = lax.psum_scatter(
        text_terms.reshape(text_rows, seq_count, 2, local_width).astype(jnp.bfloat16),
        "blk",
        scatter_dimension=0,
        tiled=True,
    ).astype(jnp.float32)
    full_kv = lax.all_gather(kv_local, "blk", axis=0, tiled=True)
    blocks = key_blocks(full_kv, shard_rows, shards, seq_count, head_count, head_dim)

    def backward_step(running, kv_block):
        partial_value, key_term = grad_block(
            query_heads,
            grad_heads,
            kv_block[:, :, 0],
            kv_block[:, :, 1],
            None,
            log_total,
            row_dot,
            score_scale,
        )
        return (running + partial_value, key_term)

    query_grads, key_terms = lax.scan(backward_step, text_query_grads, blocks)
    key_terms = key_terms.reshape(full_kv.shape[0], seq_count, 2, local_width)
    kv_grads = lax.psum_scatter(
        key_terms.astype(jnp.bfloat16), "blk", scatter_dimension=0, tiled=True
    )
    grad_projected = jnp.concatenate(
        [query_grads.astype(jnp.bfloat16).reshape(shard_rows, seq_count, 1, local_width), kv_grads],
        axis=2,
    )
    input_terms = jnp.einsum(
        "vsch,dch->vsd", grad_projected, qkv_weight, preferred_element_type=jnp.float32
    )
    grad_inputs = lax.psum_scatter(
        input_terms.astype(jnp.bfloat16), "head", scatter_dimension=2, tiled=True
    )
    qkv_part = jnp.einsum(
        "vsd,vsch->dch", full_in, grad_projected, preferred_element_type=jnp.float32
    )
    out_part = jnp.einsum("vsd,vsh->dh", full_grad, attn_out, preferred_element_type=jnp.float32)
    weight_grads = lax.psum_scatter(
        jnp.concatenate([qkv_part, out_part[:, None]], axis=1).astype(jnp.bfloat16),
        "blk",
        scatter_dimension=0,
        tiled=True,
    ).astype(jnp.float32)
    return (
        grad_inputs,
        weight_grads[:, :3],
        weight_grads[:, 3],
        text_sums[:, :, 0],
        text_sums[:, :, 1],
    )


MESH = pl.DeviceIdType.MESH
LOG2E = 1.4426950408889634
VMEM_BYTES = 60 * 1024 * 1024


def dot(a, b, contract=((1,), (0,))):
    return lax.dot_general(a, b, (contract, ((), ())), preferred_element_type=jnp.float32)


def fused_kernel(
    n,
    tile,
    x_hbm,
    g_hbm,
    wqkv_hbm,
    wout_hbm,
    tk_ref,
    tv_ref,
    mask_ref,
    dx_ref,
    dwqkv_ref,
    dwout_ref,
    dtk_ref,
    dtv_ref,
    full,
    weights,
    proj,
    ring,
    cols_in,
    cols_t,
    keys,
    values,
    keys_t,
    values_t,
    grad_k,
    grad_v,
    gp,
    pair_out,
    pair_in,
    cross_out,
    cross_in,
    load_sem,
    head_send,
    head_recv,
    ring_send,
    ring_recv,
    own_sem,
    swap_send,
    swap_recv,
    col_send,
    col_recv,
    red_send,
    red_recv,
):
    rows, depth = full.shape[1], full.shape[2]
    feats = x_hbm.shape[1]
    heads = ring.shape[0]
    text = tk_ref.shape[0]
    total_rows = ring.shape[2]
    width = cols_in.shape[3]
    quarter = rows // 4
    tiles = total_rows // tile
    half = n // 2
    scale = HD ** (-0.5)
    chunk = 512
    chunks = [(0, text)] + [(text + k * chunk, chunk) for k in range(total_rows // chunk)]

    hd = lax.axis_index("head")
    me = lax.axis_index("blk")
    sib = hd + 1 - 2 * (hd % 2)
    far = (hd + 2) % 4
    diag = (sib + 2) % 4
    odd = me % 2
    pos = (1 - odd) * (me // 2) + odd * (n - 1 - me // 2)

    def blk_at(p):
        p = p % n
        hi = p // half
        return (1 - hi) * (2 * p) + hi * (2 * (n - 1 - p) + 1)

    right, left = blk_at(pos + 1), blk_at(pos + n - 1)

    def feat(j):
        return pl.ds(pl.multiple_of(j * feats, 128), feats)

    def block(j):
        return pl.ds(pl.multiple_of(j * rows, 16), rows)

    w_loads = [
        pltpu.make_async_copy(wqkv_hbm, weights.at[pl.ds(0, 3)], load_sem.at[2]),
        pltpu.make_async_copy(wout_hbm, weights.at[3], load_sem.at[3]),
    ]
    own_loads = [
        pltpu.make_async_copy(src, full.at[a, :, feat(hd)], load_sem.at[a])
        for a, src in enumerate((x_hbm, g_hbm))
    ]
    for c in own_loads + w_loads:
        c.start()

    barrier = pltpu.get_barrier_semaphore()
    for r in range(1, n):
        pl.semaphore_signal(
            barrier, inc=1, device_id={"blk": (me + r) % n}, device_id_type=MESH
        )
    for other in (sib, far):
        pl.semaphore_signal(barrier, inc=1, device_id={"head": other}, device_id_type=MESH)
    pl.semaphore_wait(barrier, n + 1)

    def head_copy(a, kind):
        j = far if kind == 2 else hd
        ref = full.at[a, :, feat(j)]
        return pltpu.make_async_remote_copy(
            src_ref=ref,
            dst_ref=ref,
            send_sem=head_send.at[a, kind],
            recv_sem=head_recv.at[a, kind],
            device_id={"head": far if kind == 0 else sib},
            device_id_type=MESH,
        )

    own_loads[0].wait()
    head_copy(0, 0).start()
    head_copy(0, 1).start()
    own_loads[1].wait()
    head_copy(1, 1).start()

    def project(a, j, first=False):
        part = full[a, :, feat(j)]
        for c in (0, 1, 2) if a == 0 else (3,):
            term = dot(part, weights[c, feat(j), :])
            proj[c] = term if first else proj[c] + term

    def place(c):
        for h in range(heads):
            ring[h, c, block(me), :] = proj[c, :, h * HD : (h + 1) * HD].astype(jnp.bfloat16)

    def ring_copy(h, g, s, way):
        first, last = (0, 4) if h else ((0, 3), (3, 4))[g]
        if s == half:
            first, last = max(first, 2 * way), min(last, 2 * way + 2)
        if first >= last:
            return None
        p = pos - (s - 1) + n if way == 0 else pos + s - 1
        ref = ring.at[h, pl.ds(first, last - first), block(blk_at(p)), :]
        return pltpu.make_async_remote_copy(
            src_ref=ref,
            dst_ref=ref,
            send_sem=ring_send.at[h, g, s - 1, way],
            recv_sem=ring_recv.at[h, g, s - 1, way],
            device_id={"blk": right if way == 0 else left},
            device_id_type=MESH,
        )

    def hop(h, g, s):
        for way in range(2):
            if s > 1:
                ring_copy(h, g, s - 1, way).wait_recv()
            copy = ring_copy(h, g, s, way)
            if copy is not None:
                copy.start()

    def finish(h):
        for g in range(1 if h else 2):
            for way in range(2):
                for s in range(1, half + 1):
                    copy = ring_copy(h, g, s, way)
                    if copy is not None:
                        if s == half:
                            copy.wait_recv()
                        copy.wait_send()

    for c in w_loads:
        c.wait()
    project(0, hd, True)
    head_copy(0, 1).wait_recv()
    project(0, sib)
    head_copy(0, 0).wait_recv()
    head_copy(0, 2).start()
    head_copy(1, 0).start()
    project(0, far)
    head_copy(0, 2).wait_recv()
    project(0, diag)
    for c in range(3):
        place(c)
    hop(0, 0, 1)
    project(1, hd, True)
    head_copy(1, 1).wait_recv()
    project(1, sib)
    hop(0, 0, 2)
    head_copy(1, 0).wait_recv()
    head_copy(1, 2).start()
    project(1, far)
    head_copy(1, 2).wait_recv()
    project(1, diag)
    place(3)
    hop(0, 1, 1)

    mine = pl.ds(pl.multiple_of(hd * quarter, 16), quarter)

    def wide(j):
        return pl.ds(pl.multiple_of(j * width, 128), width)

    def swap_copy(r):
        to = (me + r) % n
        return pltpu.make_async_remote_copy(
            src_ref=full.at[:, mine, wide(to)],
            dst_ref=cols_in.at[:, me, mine, :],
            send_sem=swap_send.at[r],
            recv_sem=swap_recv.at[r],
            device_id={"blk": to},
            device_id_type=MESH,
        )

    own_cols = pltpu.make_async_copy(
        full.at[:, mine, wide(me)], cols_in.at[:, me, mine, :], own_sem.at[0]
    )

    def swap_start():
        own_cols.start()
        for r in range(1, n):
            swap_copy(r).start()

    def col_copy(kind):
        j = far if kind == 2 else hd
        ref = cols_in.at[:, :, pl.ds(pl.multiple_of(j * quarter, 16), quarter), :]
        return pltpu.make_async_remote_copy(
            src_ref=ref,
            dst_ref=ref,
            send_sem=col_send.at[kind],
            recv_sem=col_recv.at[kind],
            device_id={"head": far if kind == 0 else sib},
            device_id_type=MESH,
        )

    def cols_start():
        own_cols.wait()
        for r in range(1, n):
            swap_copy(r).wait_recv()
        col_copy(0).start()
        col_copy(1).start()

    def cols_forward():
        col_copy(0).wait_recv()
        col_copy(2).start()

    def attend(h, events):
        lanes = pl.ds(h * HD, HD)
        keys[pl.ds(0, text), :] = tk_ref[:, lanes]
        keys[pl.ds(text, total_rows), :] = ring[h, 1]
        values[pl.ds(0, text), :] = tv_ref[:, lanes]
        values[pl.ds(text, total_rows), :] = ring[h, 2]
        keys_t[...] = keys[...].T
        values_t[...] = values[...].T
        grad_k[...] = jnp.zeros_like(grad_k)
        grad_v[...] = jnp.zeros_like(grad_v)

        @pl.loop(0, tiles)
        def _(i):
            for at, run in events:
                pl.when(i == at)(run)
            here = pl.ds(pl.multiple_of(i * tile, tile), tile)
            q = ring[h, 0, here, :]
            go = ring[h, 3, here, :]
            q_t = q.T
            go_t = go.T
            logits = []
            top = None
            for c, (first, size) in enumerate(chunks):
                part = dot(keys[pl.ds(first, size), :], q_t)
                if c == 0:
                    part = jnp.where(mask_ref[...] > 0.0, part, masked_fill / scale)
                high = jnp.max(part, axis=0, keepdims=True)
                top = high if c == 0 else jnp.maximum(top, high)
                logits.append(part)
            top = top * (scale * LOG2E)
            weights_b = []
            total = out_t = 0.0
            for (first, size), part in zip(chunks, logits):
                p = jnp.exp2(part * (scale * LOG2E) - top)
                total = total + jnp.sum(p, axis=0, keepdims=True)
                pb = p.astype(jnp.bfloat16)
                out_t = out_t + dot(values_t[:, pl.ds(first, size)], pb)
                weights_b.append(pb)
            inv = 1.0 / total
            out_t = (out_t * inv).astype(jnp.bfloat16)
            go_s = (go_t.astype(jnp.float32) * inv).astype(jnp.bfloat16)
            row_dot = jnp.sum(
                go_s.astype(jnp.float32) * out_t.astype(jnp.float32), axis=0, keepdims=True
            )
            go_r = go_s.T

            def probs_grad(c):
                first, size = chunks[c]
                return dot(values[pl.ds(first, size), :], go_s)

            dq_t = 0.0
            ahead = probs_grad(0)
            for c, (first, size) in enumerate(chunks):
                here_k = pl.ds(first, size)
                gp_c = ahead
                if c + 1 < len(chunks):
                    ahead = probs_grad(c + 1)
                grad_v[here_k, :] += dot(weights_b[c], go_r)
                ds = weights_b[c] * (gp_c - row_dot).astype(jnp.bfloat16)
                grad_k[here_k, :] += dot(ds, q)
                dq_t = dq_t + dot(keys_t[:, here_k], ds)
            ring[h, 0, here, :] = (dq_t * scale).astype(jnp.bfloat16).T
            ring[h, 3, here, :] = out_t.T

        grad_k[...] = grad_k[...] * scale
        ring[h, 1] = grad_k[pl.ds(text, total_rows), :].astype(jnp.bfloat16)
        ring[h, 2] = grad_v[pl.ds(text, total_rows), :].astype(jnp.bfloat16)
        part = text // n
        own_text = pl.ds(pl.multiple_of(me * part, 8), part)
        dtk_ref[:, lanes] = grad_k[own_text, :]
        dtv_ref[:, lanes] = grad_v[own_text, :]

    for s in range(2, half):
        hop(0, 1, s)
        if s + 1 < half:
            hop(0, 0, s + 1)
    hop(1, 0, 1)
    hop(0, 0, half)
    hop(0, 1, half)
    early = [functools.partial(hop, 1, 0, s) for s in range(2, half + 1)]
    early.insert(1, functools.partial(hop, 2, 0, 1))
    early.append(functools.partial(hop, 2, 0, 2))
    late = [functools.partial(hop, 2, 0, s) for s in range(3, half + 1)]
    plan = [
        [(e * tiles // len(early), run) for e, run in enumerate(early)],
        [(e * tiles // (len(late) + 1), run) for e, run in enumerate(late)],
        [(1, cols_start), (tiles - 1, cols_forward)],
    ]
    plan[1].append((plan[1][-1][0], swap_start))
    for h in range(heads):
        finish(h)
        attend(h, plan[h])

    for h in range(heads):
        for c in range(3):
            gp[c, :, pl.ds(h * HD, HD)] = ring[h, c, block(me), :]

    def input_term(j):
        return sum(dot(gp[c], weights[c, feat(j), :], ((1,), (1,))) for c in range(3))

    def pair_copy(k):
        return pltpu.make_async_remote_copy(
            src_ref=pair_out.at[k],
            dst_ref=pair_in.at[k],
            send_sem=red_send.at[k],
            recv_sem=red_recv.at[k],
            device_id={"head": sib},
            device_id_type=MESH,
        )

    cross_copy = pltpu.make_async_remote_copy(
        src_ref=cross_out,
        dst_ref=cross_in,
        send_sem=red_send.at[2],
        recv_sem=red_recv.at[2],
        device_id={"head": far},
        device_id_type=MESH,
    )
    pair_out[1] = input_term(diag).astype(jnp.bfloat16)
    pair_copy(1).start()
    pair_out[0] = input_term(sib).astype(jnp.bfloat16)
    pair_copy(0).start()
    far_term = input_term(far)
    pair_copy(1).wait_recv()
    cross_out[...] = (far_term + pair_in[1].astype(jnp.float32)).astype(jnp.bfloat16)
    cross_copy.start()
    own_term = input_term(hd)
    pair_copy(0).wait_recv()
    own_term = own_term + pair_in[0].astype(jnp.float32)

    col_copy(1).wait_recv()
    col_copy(2).wait_recv()
    for a in range(2):
        cols_t[a] = cols_in[a].reshape(total_rows, width).T
    for h in range(heads):
        lanes = pl.ds(h * HD, HD)
        three = jnp.concatenate([ring[h, 0], ring[h, 1], ring[h, 2]], axis=1)
        term = dot(cols_t[0], three)
        for c in range(3):
            dwqkv_ref[c, :, lanes] = term[:, c * HD : (c + 1) * HD].astype(jnp.bfloat16)
        dwout_ref[:, lanes] = dot(cols_t[1], ring[h, 3]).astype(jnp.bfloat16)

    cross_copy.wait_recv()
    dx_ref[...] = (own_term + cross_in[...].astype(jnp.float32)).astype(jnp.bfloat16)

    for a in range(2):
        for kind in range(3):
            head_copy(a, kind).wait_send()
    for r in range(1, n):
        swap_copy(r).wait_send()
    for kind in range(3):
        col_copy(kind).wait_send()
    pair_copy(0).wait_send()
    pair_copy(1).wait_send()
    cross_copy.wait_send()


def fused_device(inputs, out_grad, qkv_weight, out_weight, text_keys, text_values, text_mask):
    n = lax.axis_size("blk")
    rows, _, feats = inputs.shape
    depth, _, local = qkv_weight.shape
    text = text_keys.shape[0]
    heads = local // HD
    total_rows = rows * n
    length = text + total_rows
    width = depth // n
    tile = 256
    bf, f32 = jnp.bfloat16, jnp.float32
    mask = jnp.broadcast_to((text_mask == 1).astype(f32), (text, tile))
    vmem = pl.BlockSpec(memory_space=pltpu.VMEM)
    hbm = pl.BlockSpec(memory_space=pl.ANY)
    dma = pltpu.SemaphoreType.DMA
    outs = pl.pallas_call(
        functools.partial(fused_kernel, n, tile),
        out_shape=(
            jax.ShapeDtypeStruct((rows, feats), bf),
            jax.ShapeDtypeStruct((3, width, local), bf),
            jax.ShapeDtypeStruct((width, local), bf),
            jax.ShapeDtypeStruct((text // n, local), f32),
            jax.ShapeDtypeStruct((text // n, local), f32),
        ),
        in_specs=[hbm] * 4 + [vmem] * 3,
        out_specs=[vmem] * 5,
        scratch_shapes=[
            pltpu.VMEM((2, rows, depth), bf),
            pltpu.VMEM((4, depth, local), bf),
            pltpu.VMEM((4, rows, local), f32),
            pltpu.VMEM((heads, 4, total_rows, HD), bf),
            pltpu.VMEM((2, n, rows, width), bf),
            pltpu.VMEM((2, width, total_rows), bf),
            pltpu.VMEM((length, HD), bf),
            pltpu.VMEM((length, HD), bf),
            pltpu.VMEM((HD, length), bf),
            pltpu.VMEM((HD, length), bf),
            pltpu.VMEM((length, HD), f32),
            pltpu.VMEM((length, HD), f32),
            pltpu.VMEM((3, rows, local), bf),
            pltpu.VMEM((2, rows, feats), bf),
            pltpu.VMEM((2, rows, feats), bf),
            pltpu.VMEM((rows, feats), bf),
            pltpu.VMEM((rows, feats), bf),
            dma((4,)),
            dma((2, 3)),
            dma((2, 3)),
            dma((heads, 2, n // 2, 2)),
            dma((heads, 2, n // 2, 2)),
            dma((1,)),
            dma((n,)),
            dma((n,)),
            dma((3,)),
            dma((3,)),
            dma((3,)),
            dma((3,)),
        ],
        compiler_params=pltpu.CompilerParams(
            collective_id=0, has_side_effects=True, vmem_limit_bytes=VMEM_BYTES
        ),
        cost_estimate=pl.CostEstimate(
            flops=2 * heads * 6 * total_rows * length * HD + 16 * rows * depth * local,
            bytes_accessed=16 * depth * local,
            transcendentals=heads * total_rows * length,
        ),
    )(
        inputs.reshape(rows, feats),
        out_grad.reshape(rows, feats),
        jnp.transpose(qkv_weight, (1, 0, 2)),
        out_weight,
        text_keys.reshape(text, local),
        text_values.reshape(text, local),
        mask,
    )
    dx, dwqkv, dwout, dtk, dtv = outs
    return (
        dx.reshape(rows, 1, feats),
        jnp.transpose(dwqkv, (1, 0, 2)).astype(f32),
        dwout.astype(f32),
        dtk.reshape(text // n, 1, local),
        dtv.reshape(text // n, 1, local),
    )


def per_device(inputs, out_grad, qkv_weight, out_weight, text_keys, text_values, text_mask):
    n = lax.axis_size("blk")
    rows, seqs, _ = inputs.shape
    depth = qkv_weight.shape[0]
    fits = (
        seqs == 1
        and lax.axis_size("head") == 4
        and n % 2 == 0
        and rows % 64 == 0
        and (rows * n) % 512 == 0
        and rows * n <= 2048
        and depth % (128 * n) == 0
        and qkv_weight.shape[2] == 3 * HD
        and n >= 8
        and text_keys.shape[0] % (8 * n) == 0
    )
    chosen = fused_device if fits else plain_device
    return chosen(inputs, out_grad, qkv_weight, out_weight, text_keys, text_values, text_mask)


def solution(mesh):
    return jax.shard_map(
        per_device,
        mesh=mesh,
        in_specs=(
            P("blk", None, "head"),
            P("blk", None, "head"),
            P(None, None, "head"),
            P(None, "head"),
            P(None, None, "head"),
            P(None, None, "head"),
            P(),
        ),
        out_specs=(
            P("blk", None, "head"),
            P("blk", None, "head"),
            P("blk", "head"),
            P("blk", None, "head"),
            P("blk", None, "head"),
        ),
        check_vma=False,
    )
```
